512 devices in a mesh: layer: 8 (over z), row: 8 (over x, core), col: 8 (over y).
Axes of the slice: x: 4, y: 8, z: 8, core: 2. Of those that a mesh axis runs over, the one named last changes fastest.
Arguments:
- rhs_low: bfloat16 [8, 2, 8, 384, 512], P('layer', None, 'col'), may hold values from -6 to 6
- inv_low: bfloat16 [8, 2, 8, 384, 384], P('layer', None, 'col'), as said below
- blocks: bfloat16 [8, 8, 8, 2, 4, 384, 384], P('layer', 'row', 'col'), may hold values from -0.02734375 to 0.02734375
- targets: int32 [8, 8, 8, 2, 4], P('layer', 'row', 'col'), may hold values from 1 to 5, as said below
- rhs_anc: bfloat16 [32, 384, 512], P('row', None, ('layer', 'col')), may hold values from -6 to 6
- inv_anc: bfloat16 [32, 384, 384], P('row'), as said below
Outputs:
- solution_low: bfloat16 [8, 2, 8, 384, 512], P('layer', None, 'col', None, 'row')
- solution_anc: float32 [32, 384, 512], P('row', None, ('layer', 'col'))
The draws below stay inside these ranges and needn't reach their ends.
Inputs may be any that keep to these rules, and one draw needn't show every extreme that they name: For each g, r, c, l the 4 values targets[g, r, c, l, :] are distinct. A value t < 2 is greater than l; a value t >= 2 names ancestor r * 4 + t - 2. `inv_low`: each block is lower triangular. `inv_anc`: each block is lower triangular.
All inputs are finite; a program needn't handle non-finite values.
Results may differ from the reference program's by a relative error of at most 0.011.
Values may be sent and summed in bfloat16 or wider, within the bound.
No kernel may reach another device: no remote copies, remote signals or barrier semaphores. Data moves between devices by JAX's collectives and lax.ppermute only.
A program may use at most 64 MiB of HBM per device.

```python
import jax
import jax.numpy as jnp
from jax import lax

W = 384
R = 512
LEVELS = 2
BPR = 4
LAYERS = 8
GRID_ROWS = 8
GRID_COLS = 8
ANC_ROW = 4
ANC = 32


def lower_block(key, count):
    first, second = jax.random.split(key)
    below = jax.random.normal(second, (count, W, W), jnp.float32) * 0.8 / jnp.sqrt(1.0 * W)
    middle = jax.random.uniform(first, (count, W), jnp.float32, 0.6, 1.4)
    return jnp.tril(below, -1) + middle[:, :, None] * jnp.eye(W, dtype=jnp.float32)[None]


def draw_inv_low(key, part):
    matrix = lower_block(jax.random.fold_in(key, 5), LAYERS * LEVELS * GRID_COLS)
    return matrix.reshape(LAYERS, LEVELS, GRID_COLS, W, W).astype(jnp.bfloat16)


def draw_inv_anc(key, part):
    matrix = lower_block(jax.random.fold_in(key, 11), ANC)
    return matrix.astype(jnp.bfloat16)


def draw_targets(key, part):
    key = jax.random.fold_in(key, 3)
    total_options = LEVELS + ANC_ROW
    full_shape = (LAYERS, GRID_ROWS, GRID_COLS, LEVELS, total_options)
    option = jnp.arange(total_options, dtype=jnp.int32).reshape(1, 1, 1, 1, -1)
    source = jnp.arange(LEVELS, dtype=jnp.int32).reshape(1, 1, 1, -1, 1)
    holder = jnp.arange(GRID_ROWS, dtype=jnp.int32).reshape(1, -1, 1, 1, 1)
    inside = (option > source) & (option < LEVELS) & (jnp.mod(holder - option, GRID_ROWS) < GRID_COLS)
    allowed = inside | (option >= LEVELS)
    scores = jax.random.randint(key, full_shape, 0, 1 << 20, dtype=jnp.int32) * total_options + option
    scores = jnp.where(allowed, scores, -1)
    picked = lax.top_k(scores, BPR)[1]
    return picked.astype(jnp.int32)


def steps_of(own_key, extent, cuts, smallest, largest):
    loudness, own = 1.0, jax.random.fold_in(own_key, 6)
    for position, shards_of in cuts:
        heights = jnp.exp(jax.random.uniform(jax.random.fold_in(own, position), (shards_of,), jnp.float32, smallest / len(cuts), largest / len(cuts)))
        loudness = loudness * jnp.repeat(heights, extent[position] // shards_of).reshape([-1 if axis == position else 1 for axis in range(len(extent))])
    return loudness


def centred(key, dims, spread, bound, cuts=(), held_as=jnp.bfloat16):
    array = jax.random.normal(key, dims, jnp.float32) * spread
    if len(cuts) > 0:
        array = steps_of(key, dims, cuts, -0.22, 0.18) * array
    return jnp.clip(array, min=-bound, max=bound).astype(held_as)


def setup_inputs(seed: int = 0) -> dict:
    keys = jax.random.split(jax.random.key(seed), 7)
    return {
        "rhs_low": centred(keys[0], (LAYERS, LEVELS, GRID_COLS, W, R), 1.0, 6.0, ((0, 8), (2, 8))),
        "inv_low": draw_inv_low(jax.random.fold_in(keys[6], 71), 0),
        "blocks": centred(keys[2], (LAYERS, GRID_ROWS, GRID_COLS, LEVELS, BPR, W, W), (128 * W) ** -0.5, 0.02734375, ((0, 8), (1, 8), (2, 8))),
        "targets": draw_targets(jax.random.fold_in(keys[6], 71), 0),
        "rhs_anc": centred(keys[4], (ANC, W, R), 1.0, 6.0, ((0, 8), (2, 64))),
        "inv_anc": draw_inv_anc(jax.random.fold_in(keys[6], 71), 0),
    }


def layer_solve(rhs_layer, inv_layer, block_layer, target_layer):
    collected = jnp.zeros((GRID_ROWS, LEVELS + ANC_ROW, W, R), jnp.float32)
    row_ids = jnp.broadcast_to(jnp.arange(GRID_ROWS, dtype=jnp.int32)[:, None, None], (GRID_ROWS, GRID_COLS, BPR))
    solved = []
    for current in range(LEVELS):
        owners = (current + jnp.arange(GRID_COLS, dtype=jnp.int32)) % GRID_ROWS
        partial_value = collected[owners, current]
        residual = (rhs_layer[current].astype(jnp.float32) - partial_value).astype(jnp.bfloat16)
        answer = jnp.einsum("cwv,cvk->cwk", inv_layer[current].astype(jnp.float32), residual.astype(jnp.float32)).astype(jnp.bfloat16)
        solved.append(answer)
        product = jnp.einsum("rcswv,cvk->rcswk", block_layer[:, :, current].astype(jnp.float32), answer.astype(jnp.float32))
        collected = collected.at[row_ids, target_layer[:, :, current]].add(product)
    return jnp.stack(solved, 0), collected[:, LEVELS:]


def reference(rhs_low, inv_low, blocks, targets, rhs_anc, inv_anc):
    def one_layer(members):
        return layer_solve(members[0], members[1], members[2], members[3])

    solution_low, ancestor_parts = lax.map(one_layer, (rhs_low, inv_low, blocks, targets))
    ancestor_partial = jnp.sum(ancestor_parts, axis=0).reshape(ANC, W, R)
    residual = (rhs_anc.astype(jnp.float32) - ancestor_partial).astype(jnp.bfloat16)
    solution_anc = jnp.einsum("awv,avk->awk", inv_anc.astype(jnp.float32), residual.astype(jnp.float32))
    return solution_low, solution_anc
```

```python
import jax
import jax.numpy as jnp
from jax import lax
from jax.experimental import pallas as pl
from jax.experimental.pallas import tpu as pltpu
from jax.sharding import PartitionSpec as P

F32 = jnp.float32
BF16 = jnp.bfloat16
NT = (((1,), (1,)), ((), ()))


def dot_nt(left, right):
    return lax.dot_general(left, right, NT, preferred_element_type=F32)


def slot_of(targets_ref, level, target, per_row):
    slot, found = jnp.int32(0), jnp.int32(0)
    for member in range(per_row):
        hit = targets_ref[level, member] == target
        slot = jnp.where(hit, jnp.int32(member), slot)
        found = jnp.where(hit, jnp.int32(1), found)
    return slot, found


def first_level(targets, place, rhs_low, inv_low, blocks, share):
    _, width, loads = rhs_low.shape
    per_row = blocks.shape[1]

    def body(targets_ref, place_ref, rhs_ref, inv_ref, block_ref, answer_ref, part_ref):
        answer = jnp.dot(inv_ref[0], rhs_ref[0], preferred_element_type=F32).T.astype(BF16)
        answer_ref[...] = answer
        _, found = slot_of(targets_ref, 0, 1, per_row)

        @pl.when(found == 1)
        def _():
            part_ref[...] = dot_nt(answer, block_ref[0, 0]).astype(BF16)

        @pl.when(found == 0)
        def _():
            part_ref[...] = jnp.zeros_like(part_ref)

    whole = lambda i, *_: (0, 0)
    return pl.pallas_call(
        body,
        out_shape=(
            jax.ShapeDtypeStruct((loads, width), BF16),
            jax.ShapeDtypeStruct((loads, width), BF16),
        ),
        grid_spec=pltpu.PrefetchScalarGridSpec(
            num_scalar_prefetch=2,
            grid=(1,),
            in_specs=[
                pl.BlockSpec((1, width, loads), lambda i, *_: (0, 0, 0)),
                pl.BlockSpec((1, width, width), lambda i, *_: (0, 0, 0)),
                pl.BlockSpec(
                    (1, 1, width, width), lambda i, t, p: (0, slot_of(t, 0, 1, per_row)[0], 0, 0)
                ),
            ],
            out_specs=(pl.BlockSpec((loads, width), whole), pl.BlockSpec((loads, width), whole)),
        ),
        compiler_params=pltpu.CompilerParams(vmem_limit_bytes=40 << 20),
        cost_estimate=pl.CostEstimate(
            flops=4 * width * width * loads, bytes_accessed=2_200_000, transcendentals=0
        ),
    )(targets, place, rhs_low, inv_low, blocks)


def second_level(place, part, rhs_low, inv_low, answer0):
    share, width = part.shape
    loads = rhs_low.shape[2]
    lanes = max(share, 128)
    per_lanes = lanes // share

    def body(place_ref, part_ref, rhs_ref, inv_ref, answer0_ref, answer_ref, both_ref):
        turned = rhs_ref[0].astype(F32).T
        right_side = turned[:share]
        for other in range(1, per_lanes):
            right_side = jnp.where(
                place_ref[0] % per_lanes == other,
                turned[other * share : (other + 1) * share],
                right_side,
            )
        residual = (right_side - part_ref[...].astype(F32)).astype(BF16)
        answer = dot_nt(residual, inv_ref[0]).astype(BF16)
        answer_ref[...] = answer
        both_ref[0] = answer0_ref[...]
        both_ref[1] = answer

    return pl.pallas_call(
        body,
        out_shape=(
            jax.ShapeDtypeStruct((share, width), BF16),
            jax.ShapeDtypeStruct((2, share, width), BF16),
        ),
        grid_spec=pltpu.PrefetchScalarGridSpec(
            num_scalar_prefetch=1,
            grid=(1,),
            in_specs=[
                pl.BlockSpec((share, width), lambda i, p: (0, 0)),
                pl.BlockSpec((1, width, lanes), lambda i, p: (1, 0, p[0] // per_lanes)),
                pl.BlockSpec((1, width, width), lambda i, p: (1, 0, 0)),
                pl.BlockSpec((share, width), lambda i, p: (p[0], 0)),
            ],
            out_specs=(
                pl.BlockSpec((share, width), lambda i, p: (0, 0)),
                pl.BlockSpec((2, share, width), lambda i, p: (0, 0, 0)),
            ),
        ),
        cost_estimate=pl.CostEstimate(
            flops=2 * width * width * share, bytes_accessed=600_000, transcendentals=0
        ),
    )(place, part, rhs_low, inv_low, answer0)


def ancestor_parts(targets, answer0, answer1, blocks):
    loads, width = answer0.shape
    per_row = blocks.shape[1]
    count = per_row

    def body(targets_ref, answer0_ref, answer1_ref, block0_ref, block1_ref, out_ref):
        target = pl.program_id(0) + 2
        _, found0 = slot_of(targets_ref, 0, target, per_row)
        _, found1 = slot_of(targets_ref, 1, target, per_row)
        keep0 = jnp.where(found0 == 1, 1.0, 0.0).astype(F32)
        keep1 = jnp.where(found1 == 1, 1.0, 0.0).astype(F32)
        total = dot_nt(answer0_ref[...], block0_ref[0, 0]) * keep0
        total += dot_nt(answer1_ref[...], block1_ref[0, 0]) * keep1
        out_ref[...] = total.astype(BF16)

    def block_spec(level):
        return pl.BlockSpec(
            (1, 1, width, width),
            lambda a, t: (level, slot_of(t, level, a + 2, per_row)[0], 0, 0),
        )

    return pl.pallas_call(
        body,
        out_shape=jax.ShapeDtypeStruct((loads, count * width), BF16),
        grid_spec=pltpu.PrefetchScalarGridSpec(
            num_scalar_prefetch=1,
            grid=(count,),
            in_specs=[
                pl.BlockSpec((loads, width), lambda a, t: (0, 0)),
                pl.BlockSpec((loads, width), lambda a, t: (0, 0)),
                block_spec(0),
                block_spec(1),
            ],
            out_specs=pl.BlockSpec((loads, width), lambda a, t: (0, a)),
        ),
        compiler_params=pltpu.CompilerParams(vmem_limit_bytes=40 << 20),
        cost_estimate=pl.CostEstimate(
            flops=4 * count * width * width * loads, bytes_accessed=5_000_000, transcendentals=0
        ),
    )(targets, answer0, answer1, blocks, blocks)


def ancestor_solve(arrived, rhs_anc, inv_anc):
    sources, loads, _ = arrived.shape
    count, _, width = rhs_anc.shape

    def body(arrived_ref, rhs_ref, inv_ref, out_ref):
        total = jnp.sum(arrived_ref[...].astype(F32), axis=0)
        residual = (rhs_ref[0].astype(F32) - total).astype(BF16)
        out_ref[0] = dot_nt(residual, inv_ref[0])

    return pl.pallas_call(
        body,
        out_shape=jax.ShapeDtypeStruct((count, loads, width), F32),
        grid=(count,),
        in_specs=[
            pl.BlockSpec((sources, loads, width), lambda a: (0, 0, a)),
            pl.BlockSpec((1, loads, width), lambda a: (a, 0, 0)),
            pl.BlockSpec((1, width, width), lambda a: (a, 0, 0)),
        ],
        out_specs=pl.BlockSpec((1, loads, width), lambda a: (a, 0, 0)),
        compiler_params=pltpu.CompilerParams(vmem_limit_bytes=40 << 20),
        cost_estimate=pl.CostEstimate(
            flops=2 * count * width * width * loads, bytes_accessed=3_000_000, transcendentals=0
        ),
    )(arrived, rhs_anc, inv_anc)


def on_device(rhs_low, inv_low, blocks, targets, rhs_anc, inv_anc):
    rows, cols = lax.axis_size("row"), lax.axis_size("col")
    rhs_low, inv_low = rhs_low[0, :, 0], inv_low[0, :, 0]
    blocks, targets = blocks[0, 0, 0], targets[0, 0, 0]
    width, loads = rhs_low.shape[1:]
    share = loads // rows
    place = lax.axis_index("row").astype(jnp.int32).reshape(1)

    answer0, part = first_level(targets, place, rhs_low, inv_low, blocks, share)
    shares = lax.all_to_all(part.reshape(cols, share, width), "col", 0, 0, tiled=True)
    summed = shares.astype(F32).sum(axis=0).astype(BF16)
    turn = [
        (row * cols + col, col * cols + (row - 1) % rows)
        for row in range(rows)
        for col in range(cols)
    ]
    summed = lax.ppermute(summed, ("row", "col"), turn)
    piece, both = second_level(place, summed, rhs_low, inv_low, answer0)
    answer1 = lax.all_gather(piece, "row", axis=0, tiled=True)

    parts = ancestor_parts(targets, answer0, answer1, blocks)
    pieces = lax.axis_size("layer") * cols
    arrived = lax.all_to_all(
        parts.reshape(pieces, loads // pieces, -1), ("layer", "col"), 0, 0, tiled=True
    )
    solved = ancestor_solve(arrived, jnp.swapaxes(rhs_anc, 1, 2), inv_anc)
    return (jnp.swapaxes(both, 1, 2)[None, :, None], jnp.swapaxes(solved, 1, 2))


def solution(mesh):
    in_specs = (
        P("layer", None, "col", None, None),
        P("layer", None, "col", None, None),
        P("layer", "row", "col", None, None, None, None),
        P("layer", "row", "col", None, None),
        P("row", None, ("layer", "col")),
        P("row", None, None),
    )
    out_specs = (P("layer", None, "col", None, "row"), P("row", None, ("layer", "col")))
    return jax.shard_map(
        on_device, mesh=mesh, in_specs=in_specs, out_specs=out_specs, check_vma=False
    )
```

```python
import jax
import jax.numpy as jnp
from jax import lax
from jax.experimental import pallas as pl
from jax.experimental.pallas import tpu as pltpu
from jax.sharding import PartitionSpec as P

F32 = jnp.float32
BF16 = jnp.bfloat16
NT = (((1,), (1,)), ((), ()))


def dot_nt(left, right):
    return lax.dot_general(left, right, NT, preferred_element_type=F32)


def slot_of(targets_ref, level, target, per_row):
    slot, found = jnp.int32(0), jnp.int32(0)
    for member in range(per_row):
        hit = targets_ref[level, member] == target
        slot = jnp.where(hit, jnp.int32(member), slot)
        found = jnp.where(hit, jnp.int32(1), found)
    return slot, found


def first_level(targets, rhs_low, inv_low, blocks, rows):
    _, width, loads = rhs_low.shape
    per_row = blocks.shape[1]
    share = loads // rows
    steps = 2
    held = rows // steps

    def body(targets_ref, rhs_ref, inv_ref, block_ref, answer_ref, part_ref):
        answer = jnp.dot(inv_ref[0], rhs_ref[0], preferred_element_type=F32).T.astype(BF16)
        for member in range(held):
            answer_ref[member % 2, member // 2] = answer[member * share : (member + 1) * share]
        _, found = slot_of(targets_ref, 0, 1, per_row)

        @pl.when(found == 1)
        def _():
            part = dot_nt(answer, block_ref[0, 0]).astype(BF16)
            part_ref[...] = part.reshape(held, share, width)

        @pl.when(found == 0)
        def _():
            part_ref[...] = jnp.zeros_like(part_ref)

    return pl.pallas_call(
        body,
        out_shape=(
            jax.ShapeDtypeStruct((2, rows // 2, share, width), BF16),
            jax.ShapeDtypeStruct((rows, share, width), BF16),
        ),
        grid_spec=pltpu.PrefetchScalarGridSpec(
            num_scalar_prefetch=1,
            grid=(steps,),
            in_specs=[
                pl.BlockSpec((1, width, loads // steps), lambda i, t: (0, 0, i)),
                pl.BlockSpec((1, width, width), lambda i, t: (0, 0, 0)),
                pl.BlockSpec(
                    (1, 1, width, width), lambda i, t: (0, slot_of(t, 0, 1, per_row)[0], 0, 0)
                ),
            ],
            out_specs=(
                pl.BlockSpec((2, held // 2, share, width), lambda i, t: (0, i, 0, 0)),
                pl.BlockSpec((held, share, width), lambda i, t: (i, 0, 0)),
            ),
        ),
        compiler_params=pltpu.CompilerParams(vmem_limit_bytes=60 << 20),
        cost_estimate=pl.CostEstimate(
            flops=4 * width * width * loads, bytes_accessed=2_200_000, transcendentals=0
        ),
    )(targets, rhs_low, inv_low, blocks)


def turned_share(place, rhs_low, level, share):
    width = rhs_low.shape[1]
    lanes = max(share, 128)
    per_lanes = lanes // share

    def body(place_ref, rhs_ref, out_ref):
        turned = rhs_ref[0].astype(F32).T
        picked = turned[:share]
        for other in range(1, per_lanes):
            picked = jnp.where(
                place_ref[0] % per_lanes == other,
                turned[other * share : (other + 1) * share],
                picked,
            )
        out_ref[...] = picked.astype(BF16)

    return pl.pallas_call(
        body,
        out_shape=jax.ShapeDtypeStruct((share, width), BF16),
        grid_spec=pltpu.PrefetchScalarGridSpec(
            num_scalar_prefetch=1,
            grid=(1,),
            in_specs=[pl.BlockSpec((1, width, lanes), lambda i, p: (level, 0, p[0] // per_lanes))],
            out_specs=pl.BlockSpec((share, width), lambda i, p: (0, 0)),
        ),
        cost_estimate=pl.CostEstimate(
            flops=width * width * 1000, bytes_accessed=2_000_000, transcendentals=0
        ),
    )(place, rhs_low)


def second_level(place, part, right_side, inv_low, answer0, copies):
    share, width = part.shape

    def body(place_ref, part_ref, rhs_ref, inv_ref, answer0_ref, answer_ref, both_ref):
        residual = (rhs_ref[...].astype(F32) - part_ref[...].astype(F32)).astype(BF16)
        answer = dot_nt(residual, inv_ref[0]).astype(BF16)
        for copy in range(copies):
            answer_ref[copy] = answer
        both_ref[0] = answer0_ref[0, 0]
        both_ref[1] = answer

    return pl.pallas_call(
        body,
        out_shape=(
            jax.ShapeDtypeStruct((copies, share, width), BF16),
            jax.ShapeDtypeStruct((2, share, width), BF16),
        ),
        grid_spec=pltpu.PrefetchScalarGridSpec(
            num_scalar_prefetch=1,
            grid=(1,),
            in_specs=[
                pl.BlockSpec((share, width), lambda i, p: (0, 0)),
                pl.BlockSpec((share, width), lambda i, p: (0, 0)),
                pl.BlockSpec((1, width, width), lambda i, p: (1, 0, 0)),
                pl.BlockSpec((1, 1, share, width), lambda i, p: (p[0] % 2, p[0] // 2, 0, 0)),
            ],
            out_specs=(
                pl.BlockSpec((copies, share, width), lambda i, p: (0, 0, 0)),
                pl.BlockSpec((2, share, width), lambda i, p: (0, 0, 0)),
            ),
        ),
        compiler_params=pltpu.CompilerParams(vmem_limit_bytes=30 << 20),
        cost_estimate=pl.CostEstimate(
            flops=2 * width * width * share, bytes_accessed=600_000, transcendentals=0
        ),
    )(place, part, right_side, inv_low, answer0)


def ancestor_parts(targets, place, answer0, answer1, blocks, flip, first, count):
    _, held, share, width = answer0.shape
    per_row = blocks.shape[1]
    loads = held * share

    def body(targets_ref, place_ref, answer0_ref, answer1_ref, block0_ref, block1_ref, out_ref):
        target = pl.program_id(0) + 2 + first
        _, found0 = slot_of(targets_ref, 0, target, per_row)
        _, found1 = slot_of(targets_ref, 1, target, per_row)
        keep0 = jnp.where(found0 == 1, 1.0, 0.0).astype(F32)
        keep1 = jnp.where(found1 == 1, 1.0, 0.0).astype(F32)
        total = dot_nt(answer0_ref[0].reshape(loads, width), block0_ref[0, 0]) * keep0
        total += dot_nt(answer1_ref[0].reshape(loads, width), block1_ref[0, 0]) * keep1
        out_ref[...] = total.astype(BF16)

    def answer_spec():
        return pl.BlockSpec((1, held, share, width), lambda a, t, p: ((p[1] + flip) % 2, 0, 0, 0))

    def block_spec(level):
        return pl.BlockSpec(
            (1, 1, width, width),
            lambda a, t, p: (level, slot_of(t, level, a + 2 + first, per_row)[0], 0, 0),
        )

    return pl.pallas_call(
        body,
        out_shape=jax.ShapeDtypeStruct((loads, count * width), BF16),
        grid_spec=pltpu.PrefetchScalarGridSpec(
            num_scalar_prefetch=2,
            grid=(count,),
            in_specs=[answer_spec(), answer_spec(), block_spec(0), block_spec(1)],
            out_specs=pl.BlockSpec((loads, width), lambda a, t, p: (0, a)),
        ),
        compiler_params=pltpu.CompilerParams(vmem_limit_bytes=30 << 20),
        cost_estimate=pl.CostEstimate(
            flops=4 * count * width * width * loads, bytes_accessed=5_000_000, transcendentals=0
        ),
    )(targets, place, answer0, answer1, blocks, blocks)


def ancestor_solve(arrived, rhs_anc, inv_anc):
    sources, loads, _ = arrived.shape
    count, _, width = rhs_anc.shape

    def body(arrived_ref, rhs_ref, inv_ref, out_ref):
        total = jnp.sum(arrived_ref[...].astype(F32), axis=0)
        residual = (rhs_ref[0].astype(F32) - total).astype(BF16)
        out_ref[0] = dot_nt(residual, inv_ref[0])

    return pl.pallas_call(
        body,
        out_shape=jax.ShapeDtypeStruct((count, loads, width), F32),
        grid=(count,),
        in_specs=[
            pl.BlockSpec((sources, loads, width), lambda a: (0, 0, a)),
            pl.BlockSpec((1, loads, width), lambda a: (a, 0, 0)),
            pl.BlockSpec((1, width, width), lambda a: (a, 0, 0)),
        ],
        out_specs=pl.BlockSpec((1, loads, width), lambda a: (a, 0, 0)),
        compiler_params=pltpu.CompilerParams(vmem_limit_bytes=40 << 20),
        cost_estimate=pl.CostEstimate(
            flops=2 * count * width * width * loads, bytes_accessed=3_000_000, transcendentals=0
        ),
    )(arrived, rhs_anc, inv_anc)


def on_device(rhs_low, inv_low, blocks, targets, rhs_anc, inv_anc):
    rows, cols = lax.axis_size("row"), lax.axis_size("col")
    rhs_low, inv_low = rhs_low[0, :, 0], inv_low[0, :, 0]
    blocks, targets = blocks[0, 0, 0], targets[0, 0, 0]
    width, loads = rhs_low.shape[1:]
    share = loads // rows
    layers, count = lax.axis_size("layer"), inv_anc.shape[0]
    place = jnp.stack([lax.axis_index("row"), lax.axis_index("layer") & 1]).astype(jnp.int32)

    answer0, part = first_level(targets, rhs_low, inv_low, blocks, rows)
    right_side = turned_share(place, rhs_low, 1, share)
    shares = lax.all_to_all(part, "col", 0, 0, tiled=True)
    summed = shares.astype(F32).sum(axis=0).astype(BF16)
    turn = [
        (row * cols + col, col * cols + (row - 1) % rows)
        for row in range(rows)
        for col in range(cols)
    ]
    summed = lax.ppermute(summed, ("row", "col"), turn)
    pieces, both = second_level(place, summed, right_side, inv_low, answer0, rows // 2)
    lines = [list(range(core, rows, 2)) for core in range(2)]
    chips = [[row, row + 1] for row in range(0, rows, 2)]
    pieces = lax.all_to_all(pieces, "row", 0, 0, axis_index_groups=lines, tiled=True)
    answer1 = lax.all_gather(pieces, "row", axis=0, axis_index_groups=chips)

    half = count // 2
    near = [(layer, layer ^ 1) for layer in range(layers)]
    far = [(layer, (layer + (1 if layer % 2 else -1)) % layers) for layer in range(layers)]
    give_near = ancestor_parts(targets, place, answer0, answer1, blocks, 1, 0, half)
    got_near = lax.ppermute(give_near, "layer", near)
    give_far = ancestor_parts(targets, place, answer0, answer1, blocks, 1, half, count - half)
    got_far = lax.ppermute(give_far, "layer", far)
    kept = ancestor_parts(targets, place, answer0, answer1, blocks, 0, 0, count)
    got = jnp.concatenate([got_near, got_far], axis=1)
    parts = (kept.astype(F32) + got.astype(F32)).astype(BF16)
    groups = [
        [layer * cols + col for layer in range(parity, layers, 2) for col in range(cols)]
        for parity in range(2)
    ]
    members = len(groups[0])
    arrived = lax.all_to_all(
        parts.reshape(members, parts.shape[0] // members, -1),
        ("layer", "col"),
        0,
        0,
        axis_index_groups=groups,
        tiled=True,
    )
    solved = ancestor_solve(arrived, jnp.swapaxes(rhs_anc, 1, 2), inv_anc)
    return (jnp.swapaxes(both, 1, 2)[None, :, None], jnp.swapaxes(solved, 1, 2))


def solution(mesh):
    in_specs = (
        P("layer", None, "col", None, None),
        P("layer", None, "col", None, None),
        P("layer", "row", "col", None, None, None, None),
        P("layer", "row", "col", None, None),
        P("row", None, ("layer", "col")),
        P("row", None, None),
    )
    out_specs = (P("layer", None, "col", None, "row"), P("row", None, ("layer", "col")))
    return jax.shard_map(
        on_device, mesh=mesh, in_specs=in_specs, out_specs=out_specs, check_vma=False
    )
```

```python
import jax
import jax.numpy as jnp
from jax import lax
from jax.experimental import pallas as pl
from jax.experimental.pallas import tpu as pltpu
from jax.sharding import PartitionSpec as P

F32 = jnp.float32
BF16 = jnp.bfloat16
SMALL = 8 << 20
LARGE = 24 << 20
FIRST = 60 << 20
NT = (((1,), (1,)), ((), ()))


def dot_nt(left, right):
    return lax.dot_general(left, right, NT, preferred_element_type=F32)


def slot_of(targets_ref, level, target, per_row):
    slot, found = jnp.int32(0), jnp.int32(0)
    for member in range(per_row):
        hit = targets_ref[level, member] == target
        slot = jnp.where(hit, jnp.int32(member), slot)
        found = jnp.where(hit, jnp.int32(1), found)
    return slot, found


def first_level(targets, rhs_low, inv_low, blocks, rows):
    _, width, loads = rhs_low.shape
    per_row = blocks.shape[1]
    share = loads // rows
    steps = 2
    held = rows // steps

    def body(targets_ref, rhs_ref, inv_ref, block_ref, answer_ref, part_ref):
        answer = jnp.dot(inv_ref[0], rhs_ref[0], preferred_element_type=F32).T.astype(BF16)
        for member in range(held):
            answer_ref[member % 2, member // 2] = answer[member * share : (member + 1) * share]
        _, found = slot_of(targets_ref, 0, 1, per_row)

        @pl.when(found == 1)
        def _():
            part = dot_nt(answer, block_ref[0, 0]).astype(BF16)
            part_ref[...] = part.reshape(held, share, width)

        @pl.when(found == 0)
        def _():
            part_ref[...] = jnp.zeros_like(part_ref)

    return pl.pallas_call(
        body,
        out_shape=(
            jax.ShapeDtypeStruct((2, rows // 2, share, width), BF16),
            jax.ShapeDtypeStruct((rows, share, width), BF16),
        ),
        grid_spec=pltpu.PrefetchScalarGridSpec(
            num_scalar_prefetch=1,
            grid=(steps,),
            in_specs=[
                pl.BlockSpec((1, width, loads // steps), lambda i, t: (0, 0, i)),
                pl.BlockSpec((1, width, width), lambda i, t: (0, 0, 0)),
                pl.BlockSpec(
                    (1, 1, width, width), lambda i, t: (0, slot_of(t, 0, 1, per_row)[0], 0, 0)
                ),
            ],
            out_specs=(
                pl.BlockSpec((2, held // 2, share, width), lambda i, t: (0, i, 0, 0)),
                pl.BlockSpec((held, share, width), lambda i, t: (i, 0, 0)),
            ),
        ),
        compiler_params=pltpu.CompilerParams(vmem_limit_bytes=FIRST),
        cost_estimate=pl.CostEstimate(
            flops=4 * width * width * loads, bytes_accessed=2_200_000, transcendentals=0
        ),
    )(targets, rhs_low, inv_low, blocks)


def turned_shares(rhs_low, level, rows):
    _, width, loads = rhs_low.shape
    share = loads // rows
    steps = 2
    held = rows // steps

    def body(rhs_ref, out_ref):
        turned = rhs_ref[0].astype(F32).T.astype(BF16)
        for member in range(held):
            out_ref[member % 2, member // 2] = turned[member * share : (member + 1) * share]

    return pl.pallas_call(
        body,
        out_shape=jax.ShapeDtypeStruct((2, rows // 2, share, width), BF16),
        grid=(steps,),
        in_specs=[pl.BlockSpec((1, width, loads // steps), lambda i: (level, 0, i))],
        out_specs=pl.BlockSpec((2, held // 2, share, width), lambda i: (0, i, 0, 0)),
        compiler_params=pltpu.CompilerParams(vmem_limit_bytes=SMALL),
        cost_estimate=pl.CostEstimate(
            flops=width * width * 1000, bytes_accessed=2_000_000, transcendentals=0
        ),
    )(rhs_low)


def second_level(place, parts, right_sides, inv_low):
    hops = len(parts)
    share, width = parts[0].shape

    def body(place_ref, *refs):
        parts_refs, (rhs_ref, inv_ref, answer_ref) = refs[:hops], refs[hops:]
        for hop in range(hops):
            spot = (place_ref[0] // 2 + hops - hop) % hops
            residual = (rhs_ref[0, spot].astype(F32) - parts_refs[hop][...].astype(F32)).astype(BF16)
            answer_ref[spot] = dot_nt(residual, inv_ref[0]).astype(BF16)

    return pl.pallas_call(
        body,
        out_shape=jax.ShapeDtypeStruct((hops, share, width), BF16),
        grid_spec=pltpu.PrefetchScalarGridSpec(
            num_scalar_prefetch=1,
            grid=(1,),
            in_specs=[pl.BlockSpec((share, width), lambda i, p: (0, 0))] * hops
            + [
                pl.BlockSpec((1, hops, share, width), lambda i, p: (p[0] % 2, 0, 0, 0)),
                pl.BlockSpec((1, width, width), lambda i, p: (1, 0, 0)),
            ],
            out_specs=pl.BlockSpec((hops, share, width), lambda i, p: (0, 0, 0)),
        ),
        compiler_params=pltpu.CompilerParams(vmem_limit_bytes=SMALL),
        cost_estimate=pl.CostEstimate(
            flops=2 * width * width * share * hops, bytes_accessed=900_000, transcendentals=0
        ),
    )(place, *parts, right_sides, inv_low)


def ancestor_parts(targets, place, answer0, answer1, blocks, flip, first, count):
    _, held, share, width = answer0.shape
    per_row = blocks.shape[1]
    loads = held * share

    def body(targets_ref, place_ref, answer0_ref, answer1_ref, block0_ref, block1_ref, out_ref):
        target = pl.program_id(0) + 2 + first
        _, found0 = slot_of(targets_ref, 0, target, per_row)
        _, found1 = slot_of(targets_ref, 1, target, per_row)
        keep0 = jnp.where(found0 == 1, 1.0, 0.0).astype(F32)
        keep1 = jnp.where(found1 == 1, 1.0, 0.0).astype(F32)
        total = dot_nt(answer0_ref[0].reshape(loads, width), block0_ref[0, 0]) * keep0
        total += dot_nt(answer1_ref[0].reshape(loads, width), block1_ref[0, 0]) * keep1
        out_ref[...] = total.astype(BF16)

    def answer_spec():
        return pl.BlockSpec((1, held, share, width), lambda a, t, p: ((p[1] + flip) % 2, 0, 0, 0))

    def block_spec(level):
        return pl.BlockSpec(
            (1, 1, width, width),
            lambda a, t, p: (level, slot_of(t, level, a + 2 + first, per_row)[0], 0, 0),
        )

    return pl.pallas_call(
        body,
        out_shape=jax.ShapeDtypeStruct((loads, count * width), BF16),
        grid_spec=pltpu.PrefetchScalarGridSpec(
            num_scalar_prefetch=2,
            grid=(count,),
            in_specs=[answer_spec(), answer_spec(), block_spec(0), block_spec(1)],
            out_specs=pl.BlockSpec((loads, width), lambda a, t, p: (0, a)),
        ),
        compiler_params=pltpu.CompilerParams(vmem_limit_bytes=LARGE),
        cost_estimate=pl.CostEstimate(
            flops=4 * count * width * width * loads, bytes_accessed=5_000_000, transcendentals=0
        ),
    )(targets, place, answer0, answer1, blocks, blocks)


def ancestor_solve(place, arrived, rhs_anc, inv_anc, answer0, answer1):
    sources, loads, _ = arrived.shape
    count, _, width = rhs_anc.shape
    share = answer0.shape[2]

    def body(place_ref, arrived_ref, rhs_ref, inv_ref, answer0_ref, answer1_ref, out_ref, both_ref):
        total = jnp.sum(arrived_ref[...].astype(F32), axis=0)
        residual = (rhs_ref[0].astype(F32) - total).astype(BF16)
        out_ref[0] = dot_nt(residual, inv_ref[0])

        @pl.when(pl.program_id(0) == 0)
        def _():
            both_ref[0] = answer0_ref[0, 0]
            both_ref[1] = answer1_ref[0, 0]

    own = pl.BlockSpec((1, 1, share, width), lambda a, p: (p[0] % 2, p[0] // 2, 0, 0))
    return pl.pallas_call(
        body,
        out_shape=(
            jax.ShapeDtypeStruct((count, loads, width), F32),
            jax.ShapeDtypeStruct((2, share, width), BF16),
        ),
        grid_spec=pltpu.PrefetchScalarGridSpec(
            num_scalar_prefetch=1,
            grid=(count,),
            in_specs=[
                pl.BlockSpec((sources, loads, width), lambda a, p: (0, 0, a)),
                pl.BlockSpec((1, loads, width), lambda a, p: (a, 0, 0)),
                pl.BlockSpec((1, width, width), lambda a, p: (a, 0, 0)),
                own,
                own,
            ],
            out_specs=(
                pl.BlockSpec((1, loads, width), lambda a, p: (a, 0, 0)),
                pl.BlockSpec((2, share, width), lambda a, p: (0, 0, 0)),
            ),
        ),
        compiler_params=pltpu.CompilerParams(vmem_limit_bytes=LARGE),
        cost_estimate=pl.CostEstimate(
            flops=2 * count * width * width * loads, bytes_accessed=3_000_000, transcendentals=0
        ),
    )(place, arrived, rhs_anc, inv_anc, answer0, answer1)


def on_device(rhs_low, inv_low, blocks, targets, rhs_anc, inv_anc):
    rows, cols = lax.axis_size("row"), lax.axis_size("col")
    rhs_low, inv_low = rhs_low[0, :, 0], inv_low[0, :, 0]
    blocks, targets = blocks[0, 0, 0], targets[0, 0, 0]
    width, loads = rhs_low.shape[1:]
    layers, count = lax.axis_size("layer"), inv_anc.shape[0]
    place = jnp.stack([lax.axis_index("row"), lax.axis_index("layer") & 1]).astype(jnp.int32)

    answer0, part = first_level(targets, rhs_low, inv_low, blocks, rows)
    right_sides = turned_shares(rhs_low, 1, rows)
    shares = lax.all_to_all(part, "col", 0, 0, tiled=True)
    summed = shares.astype(F32).sum(axis=0).astype(BF16)
    hops = rows // 2
    arrived = [
        lax.ppermute(
            summed,
            ("row", "col"),
            [
                (row * cols + col, ((col // 2 + hop) % hops * 2 + col % 2) * cols + (row - 1) % rows)
                for row in range(rows)
                for col in range(cols)
            ],
        )
        for hop in range(hops)
    ]
    solved = second_level(place, arrived, right_sides, inv_low)
    chips = [[row, row + 1] for row in range(0, rows, 2)]
    answer1 = lax.all_gather(solved, "row", axis=0, axis_index_groups=chips)

    half = count // 2
    near = [(layer, layer ^ 1) for layer in range(layers)]
    far = [(layer, (layer + (1 if layer % 2 else -1)) % layers) for layer in range(layers)]
    give_near = ancestor_parts(targets, place, answer0, answer1, blocks, 1, 0, half)
    got_near = lax.ppermute(give_near, "layer", near)
    give_far = ancestor_parts(targets, place, answer0, answer1, blocks, 1, half, count - half)
    got_far = lax.ppermute(give_far, "layer", far)
    kept = ancestor_parts(targets, place, answer0, answer1, blocks, 0, 0, count)
    got = jnp.concatenate([got_near, got_far], axis=1)
    parts = (kept.astype(F32) + got.astype(F32)).astype(BF16)
    groups = [
        [layer * cols + col for layer in range(parity, layers, 2) for col in range(cols)]
        for parity in range(2)
    ]
    members = len(groups[0])
    arrived = lax.all_to_all(
        parts.reshape(members, parts.shape[0] // members, -1),
        ("layer", "col"),
        0,
        0,
        axis_index_groups=groups,
        tiled=True,
    )
    solved, both = ancestor_solve(
        place, arrived, jnp.swapaxes(rhs_anc, 1, 2), inv_anc, answer0, answer1
    )
    return (jnp.swapaxes(both, 1, 2)[None, :, None], jnp.swapaxes(solved, 1, 2))


def solution(mesh):
    in_specs = (
        P("layer", None, "col", None, None),
        P("layer", None, "col", None, None),
        P("layer", "row", "col", None, None, None, None),
        P("layer", "row", "col", None, None),
        P("row", None, ("layer", "col")),
        P("row", None, None),
    )
    out_specs = (P("layer", None, "col", None, "row"), P("row", None, ("layer", "col")))
    return jax.shard_map(
        on_device, mesh=mesh, in_specs=in_specs, out_specs=out_specs, check_vma=False
    )
```

```python
import jax
import jax.numpy as jnp
from jax import lax
from jax.experimental import pallas as pl
from jax.experimental.pallas import tpu as pltpu
from jax.sharding import PartitionSpec as P

F32 = jnp.float32
BF16 = jnp.bfloat16
SMALL = 8 << 20
LARGE = 24 << 20
FIRST = 60 << 20
NT = (((1,), (1,)), ((), ()))


def dot_nt(left, right):
    return lax.dot_general(left, right, NT, preferred_element_type=F32)


def slot_of(targets_ref, level, target, per_row):
    slot, found = jnp.int32(0), jnp.int32(0)
    for member in range(per_row):
        hit = targets_ref[level, member] == target
        slot = jnp.where(hit, jnp.int32(member), slot)
        found = jnp.where(hit, jnp.int32(1), found)
    return slot, found


def first_level(targets, rhs_low, inv_low, blocks, rows):
    levels, width, loads = rhs_low.shape
    per_row = blocks.shape[1]
    share = loads // rows
    steps = 2
    held = rows // steps
    half = rows // 2

    def body(targets_ref, rhs_ref, inv_ref, block_ref, answer_ref, part_ref, give_ref):
        step = pl.program_id(0)
        kept = lax.axis_index("layer") % 2
        answer = jnp.dot(inv_ref[0], rhs_ref[0], preferred_element_type=F32).T.astype(BF16)
        pieces = [answer[member * share : (member + 1) * share] for member in range(held)]
        for member in range(held):
            answer_ref[member % 2, member // 2] = pieces[member]
        for parity in range(2):

            @pl.when(kept == 1 - parity)
            def _(parity=parity):
                for member in range(parity, held, 2):
                    give_ref[step * (held // 2) + member // 2] = pieces[member]

        @pl.when(step == 0)
        def _():
            row = lax.broadcasted_iota(jnp.int32, (share, width), 0)
            table = jnp.zeros((share, width), F32)
            for level in range(levels):
                for member in range(per_row):
                    value = targets_ref[level, member].astype(F32)
                    table = jnp.where(row == level * per_row + member, value, table)
            give_ref[half] = table.astype(BF16)

        _, found = slot_of(targets_ref, 0, 1, per_row)

        @pl.when(found == 1)
        def _():
            part = dot_nt(answer, block_ref[0, 0]).astype(BF16)
            part_ref[...] = part.reshape(held, share, width)

        @pl.when(found == 0)
        def _():
            part_ref[...] = jnp.zeros_like(part_ref)

    return pl.pallas_call(
        body,
        out_shape=(
            jax.ShapeDtypeStruct((2, half, share, width), BF16),
            jax.ShapeDtypeStruct((rows, share, width), BF16),
            jax.ShapeDtypeStruct((half + 1, share, width), BF16),
        ),
        grid_spec=pltpu.PrefetchScalarGridSpec(
            num_scalar_prefetch=1,
            grid=(steps,),
            in_specs=[
                pl.BlockSpec((1, width, loads // steps), lambda i, t: (0, 0, i)),
                pl.BlockSpec((1, width, width), lambda i, t: (0, 0, 0)),
                pl.BlockSpec(
                    (1, 1, width, width), lambda i, t: (0, slot_of(t, 0, 1, per_row)[0], 0, 0)
                ),
            ],
            out_specs=(
                pl.BlockSpec((2, held // 2, share, width), lambda i, t: (0, i, 0, 0)),
                pl.BlockSpec((held, share, width), lambda i, t: (i, 0, 0)),
                pl.BlockSpec((half + 1, share, width), lambda i, t: (0, 0, 0)),
            ),
        ),
        compiler_params=pltpu.CompilerParams(vmem_limit_bytes=FIRST),
        cost_estimate=pl.CostEstimate(
            flops=4 * width * width * loads, bytes_accessed=2_200_000, transcendentals=0
        ),
    )(targets, rhs_low, inv_low, blocks)


def turned_share(place, rhs_low, level, share):
    width = rhs_low.shape[1]
    lanes = max(share, 128)
    per_lanes = lanes // share

    def body(place_ref, rhs_ref, out_ref):
        turned = rhs_ref[0].astype(F32).T
        picked = turned[:share]
        for other in range(1, per_lanes):
            picked = jnp.where(
                place_ref[0] % per_lanes == other,
                turned[other * share : (other + 1) * share],
                picked,
            )
        out_ref[...] = picked.astype(BF16)

    return pl.pallas_call(
        body,
        out_shape=jax.ShapeDtypeStruct((share, width), BF16),
        grid_spec=pltpu.PrefetchScalarGridSpec(
            num_scalar_prefetch=1,
            grid=(1,),
            in_specs=[pl.BlockSpec((1, width, lanes), lambda i, p: (level, 0, p[0] // per_lanes))],
            out_specs=pl.BlockSpec((share, width), lambda i, p: (0, 0)),
        ),
        compiler_params=pltpu.CompilerParams(vmem_limit_bytes=SMALL),
        cost_estimate=pl.CostEstimate(
            flops=width * width * 1000, bytes_accessed=2_000_000, transcendentals=0
        ),
    )(place, rhs_low)


def second_level(place, part, right_side, inv_low, answer0, copies):
    share, width = part.shape

    def body(place_ref, part_ref, rhs_ref, inv_ref, answer0_ref, answer_ref, both_ref):
        residual = (rhs_ref[...].astype(F32) - part_ref[...].astype(F32)).astype(BF16)
        answer = dot_nt(residual, inv_ref[0]).astype(BF16)
        for copy in range(copies):
            answer_ref[copy] = answer
        both_ref[0] = answer0_ref[0, 0]
        both_ref[1] = answer

    return pl.pallas_call(
        body,
        out_shape=(
            jax.ShapeDtypeStruct((copies, share, width), BF16),
            jax.ShapeDtypeStruct((2, share, width), BF16),
        ),
        grid_spec=pltpu.PrefetchScalarGridSpec(
            num_scalar_prefetch=1,
            grid=(1,),
            in_specs=[
                pl.BlockSpec((share, width), lambda i, p: (0, 0)),
                pl.BlockSpec((share, width), lambda i, p: (0, 0)),
                pl.BlockSpec((1, width, width), lambda i, p: (1, 0, 0)),
                pl.BlockSpec((1, 1, share, width), lambda i, p: (p[0] % 2, p[0] // 2, 0, 0)),
            ],
            out_specs=(
                pl.BlockSpec((copies, share, width), lambda i, p: (0, 0, 0)),
                pl.BlockSpec((2, share, width), lambda i, p: (0, 0, 0)),
            ),
        ),
        compiler_params=pltpu.CompilerParams(vmem_limit_bytes=FIRST),
        cost_estimate=pl.CostEstimate(
            flops=2 * width * width * share, bytes_accessed=600_000, transcendentals=0
        ),
    )(place, part, right_side, inv_low, answer0)


def ancestor_parts(targets, place, own, near, table, before=None):
    _, count, width, _ = near[0][1].shape
    held, share = table.shape[0] - 1, table.shape[1]
    loads = held * share
    terms = len(own) + len(near)

    def body(targets_ref, place_ref, *refs):
        answers, blocks = refs[:terms], refs[terms : 2 * terms]
        table_ref, out_ref = refs[2 * terms], refs[-1]
        target = pl.program_id(0) + 2
        total = None
        for index in range(terms):
            if index < len(own):
                _, found = slot_of(targets_ref, own[index][0], target, count)
                value = answers[index][0].reshape(loads, width)
                product = dot_nt(value, blocks[index][0, 0])
                product = product * jnp.where(found == 1, 1.0, 0.0).astype(F32)
            else:
                level = near[index - len(own)][0]
                lists = table_ref[0].astype(F32)
                block = jnp.zeros((width, width), BF16)
                for member in range(count):
                    named = lists[level * count + member :][:1] == target.astype(F32)
                    block += blocks[index][0, member] * jnp.where(named, 1.0, 0.0).astype(BF16)
                value = answers[index][:held].reshape(loads, width)
                product = dot_nt(value, block)
            total = product if total is None else total + product
        if before is not None:
            total += refs[2 * terms + 1][...].astype(F32)
        out_ref[...] = total.astype(BF16)

    def own_block(level):
        return pl.BlockSpec(
            (1, 1, width, width),
            lambda a, t, p: (level, slot_of(t, level, a + 2, count)[0], 0, 0),
        )

    def near_block(level):
        return pl.BlockSpec((1, count, width, width), lambda a, t, p: (level, 0, 0, 0))

    def near_answer(answer):
        return pl.BlockSpec(answer.shape, lambda a, t, p: (0, 0, 0))

    out_spec = pl.BlockSpec((loads, width), lambda a, t, p: (0, a))
    in_specs = [pl.BlockSpec((1, held, share, width), lambda a, t, p: (p[1], 0, 0, 0)) for _ in own]
    in_specs += [near_answer(term[2]) for term in near]
    in_specs += [own_block(term[0]) for term in own] + [near_block(term[0]) for term in near]
    in_specs.append(pl.BlockSpec((1, share, width), lambda a, t, p: (held, 0, 0)))
    operands = [term[2] for term in (*own, *near)] + [term[1] for term in (*own, *near)] + [table]
    if before is not None:
        in_specs.append(out_spec)
        operands.append(before)
    return pl.pallas_call(
        body,
        out_shape=jax.ShapeDtypeStruct((loads, count * width), BF16),
        grid_spec=pltpu.PrefetchScalarGridSpec(
            num_scalar_prefetch=2, grid=(count,), in_specs=in_specs, out_specs=out_spec
        ),
        compiler_params=pltpu.CompilerParams(vmem_limit_bytes=LARGE),
        cost_estimate=pl.CostEstimate(
            flops=2 * terms * count * width * width * loads,
            bytes_accessed=5_000_000,
            transcendentals=0,
        ),
    )(targets, place, *operands)


def ancestor_solve(arrived, rhs_anc, inv_anc):
    sources, loads, _ = arrived.shape
    count, _, width = rhs_anc.shape

    def body(arrived_ref, rhs_ref, inv_ref, out_ref):
        total = jnp.sum(arrived_ref[...].astype(F32), axis=0)
        residual = (rhs_ref[0].astype(F32) - total).astype(BF16)
        out_ref[0] = dot_nt(residual, inv_ref[0])

    return pl.pallas_call(
        body,
        out_shape=jax.ShapeDtypeStruct((count, loads, width), F32),
        grid=(count,),
        in_specs=[
            pl.BlockSpec((sources, loads, width), lambda a: (0, 0, a)),
            pl.BlockSpec((1, loads, width), lambda a: (a, 0, 0)),
            pl.BlockSpec((1, width, width), lambda a: (a, 0, 0)),
        ],
        out_specs=pl.BlockSpec((1, loads, width), lambda a: (a, 0, 0)),
        compiler_params=pltpu.CompilerParams(vmem_limit_bytes=LARGE),
        cost_estimate=pl.CostEstimate(
            flops=2 * count * width * width * loads, bytes_accessed=3_000_000, transcendentals=0
        ),
    )(arrived, rhs_anc, inv_anc)


def on_device(rhs_low, inv_low, blocks, targets, rhs_anc, inv_anc):
    rows, cols = lax.axis_size("row"), lax.axis_size("col")
    rhs_low, inv_low = rhs_low[0, :, 0], inv_low[0, :, 0]
    blocks, targets = blocks[0, 0, 0], targets[0, 0, 0]
    width, loads = rhs_low.shape[1:]
    layers, share = lax.axis_size("layer"), loads // rows
    place = jnp.stack([lax.axis_index("row"), lax.axis_index("layer") & 1]).astype(jnp.int32)

    answer0, part, give0 = first_level(targets, rhs_low, inv_low, blocks, rows)
    right_side = turned_share(place, rhs_low, 1, share)
    shares = lax.all_to_all(part, "col", 0, 0, tiled=True)

    def neighbour(layer, row):
        ahead = (layer + row) % 2 == 0
        return (layer + (1 if ahead else -1)) % layers

    pairs = [
        (layer * rows + row, neighbour(layer, row) * rows + row)
        for layer in range(layers)
        for row in range(rows)
    ]

    def swap(value):
        return lax.ppermute(value, ("layer", "row"), pairs)

    near_blocks, near_answer0 = swap(blocks), swap(give0)

    summed = shares.astype(F32).sum(axis=0).astype(BF16)
    turn = [
        (row * cols + col, col * cols + (row - 1) % rows)
        for row in range(rows)
        for col in range(cols)
    ]
    summed = lax.ppermute(summed, ("row", "col"), turn)
    pieces, both = second_level(place, summed, right_side, inv_low, answer0, rows // 2)
    lines = [list(range(core, rows, 2)) for core in range(2)]
    chips = [[row, row + 1] for row in range(0, rows, 2)]
    pieces = lax.all_to_all(pieces, "row", 0, 0, axis_index_groups=lines, tiled=True)
    answer1 = lax.all_gather(pieces, "row", axis=0, axis_index_groups=chips)

    near_answer1 = swap(lax.dynamic_index_in_dim(answer1, 1 - place[1], 0, keepdims=False))
    own = [(0, blocks, answer0), (1, blocks, answer1)]
    parts = ancestor_parts(targets, place, own, [(0, near_blocks, near_answer0)], near_answer0)
    late = [(1, near_blocks, near_answer1)]
    parts = ancestor_parts(targets, place, [], late, near_answer0, parts)
    groups = [
        [layer * cols + col for layer in range(parity, layers, 2) for col in range(cols)]
        for parity in range(2)
    ]
    members = len(groups[0])
    arrived = lax.all_to_all(
        parts.reshape(members, parts.shape[0] // members, -1),
        ("layer", "col"),
        0,
        0,
        axis_index_groups=groups,
        tiled=True,
    )
    solved = ancestor_solve(arrived, jnp.swapaxes(rhs_anc, 1, 2), inv_anc)
    return (jnp.swapaxes(both, 1, 2)[None, :, None], jnp.swapaxes(solved, 1, 2))


def solution(mesh):
    in_specs = (
        P("layer", None, "col", None, None),
        P("layer", None, "col", None, None),
        P("layer", "row", "col", None, None, None, None),
        P("layer", "row", "col", None, None),
        P("row", None, ("layer", "col")),
        P("row", None, None),
    )
    out_specs = (P("layer", None, "col", None, "row"), P("row", None, ("layer", "col")))
    return jax.shard_map(
        on_device, mesh=mesh, in_specs=in_specs, out_specs=out_specs, check_vma=False
    )
```

```python
import jax
import jax.numpy as jnp
from jax import lax
from jax.experimental import pallas as pl
from jax.experimental.pallas import tpu as pltpu
from jax.sharding import PartitionSpec as P

F32 = jnp.float32
BF16 = jnp.bfloat16
SMALL = 8 << 20
LARGE = 24 << 20
FIRST = 60 << 20
NT = (((1,), (1,)), ((), ()))


def dot_nt(left, right):
    return lax.dot_general(left, right, NT, preferred_element_type=F32)


def slot_of(targets_ref, level, target, per_row):
    slot, found = jnp.int32(0), jnp.int32(0)
    for member in range(per_row):
        hit = targets_ref[level, member] == target
        slot = jnp.where(hit, jnp.int32(member), slot)
        found = jnp.where(hit, jnp.int32(1), found)
    return slot, found


def first_level(targets, rhs_low, inv_low, blocks, rows):
    levels, width, loads = rhs_low.shape
    per_row = blocks.shape[1]
    share = loads // rows
    steps = 2
    held, half = rows // steps, rows // 2
    slots = levels * per_row

    def body(
        targets_ref, rhs_ref, inv_ref, blocks_ref, answer_ref, part_ref, give_ref,
        rhs_in, inv_in, block_in, zeros, half_out, in_sems, out_sems,
    ):
        kept = lax.axis_index("layer") % 2
        slot, found = slot_of(targets_ref, 0, 1, per_row)
        inv_copy = pltpu.make_async_copy(inv_ref.at[0], inv_in, in_sems.at[steps])
        block_copy = pltpu.make_async_copy(blocks_ref.at[0, slot], block_in, in_sems.at[steps + 1])
        rhs_copies = [
            pltpu.make_async_copy(
                rhs_ref.at[0, :, pl.ds(step * (loads // steps), loads // steps)],
                rhs_in.at[step],
                in_sems.at[step],
            )
            for step in range(steps)
        ]
        inv_copy.start()
        for copy in rhs_copies:
            copy.start()
        block_copy.start()
        zeros[...] = jnp.zeros_like(zeros)

        def give(index):
            return give_ref.at[pl.ds(index * width, width)]

        for index in range(slots):
            level, ancestor = index // per_row, index % per_row
            source, named = slot_of(targets_ref, level, ancestor + 2, per_row)

            @pl.when(named == 1)
            def _(index=index, level=level, source=source):
                pltpu.make_async_copy(
                    blocks_ref.at[level, source], give(index), out_sems.at[index]
                ).start()

            @pl.when(named == 0)
            def _(index=index):
                pltpu.make_async_copy(zeros, give(index), out_sems.at[index]).start()

        inv_copy.wait()
        answers = []
        for step in range(steps):
            rhs_copies[step].wait()
            answer = jnp.dot(inv_in[...], rhs_in[step], preferred_element_type=F32).T.astype(BF16)
            answers.append(answer)
            pieces = [answer[member * share : (member + 1) * share] for member in range(held)]
            for member in range(held):
                answer_ref[member % 2, step * (held // 2) + member // 2] = pieces[member]
            for member in range(0, held, 2):
                start = (step * (held // 2) + member // 2) * share

                @pl.when(kept == 1)
                def _(start=start, piece=pieces[member]):
                    half_out[start : start + share] = piece

                @pl.when(kept == 0)
                def _(start=start, piece=pieces[member + 1]):
                    half_out[start : start + share] = piece

        half_copy = pltpu.make_async_copy(
            half_out, give_ref.at[pl.ds(slots * width, half * share)], out_sems.at[slots]
        )
        half_copy.start()
        block_copy.wait()

        @pl.when(found == 1)
        def _():
            for step in range(steps):
                part = dot_nt(answers[step], block_in[...]).astype(BF16)
                part_ref[step * held : (step + 1) * held] = part.reshape(held, share, width)

        @pl.when(found == 0)
        def _():
            part_ref[...] = jnp.zeros_like(part_ref)

        for index in range(slots):
            pltpu.make_async_copy(zeros, give(index), out_sems.at[index]).wait()
        half_copy.wait()

    any_spec, vmem = pl.BlockSpec(memory_space=pl.ANY), pl.BlockSpec(memory_space=pltpu.VMEM)
    return pl.pallas_call(
        body,
        out_shape=(
            jax.ShapeDtypeStruct((2, half, share, width), BF16),
            jax.ShapeDtypeStruct((rows, share, width), BF16),
            jax.ShapeDtypeStruct((slots * width + half * share, width), BF16),
        ),
        in_specs=[pl.BlockSpec(memory_space=pltpu.SMEM), any_spec, any_spec, any_spec],
        out_specs=(vmem, vmem, any_spec),
        scratch_shapes=[
            pltpu.VMEM((steps, width, loads // steps), BF16),
            pltpu.VMEM((width, width), BF16),
            pltpu.VMEM((width, width), BF16),
            pltpu.VMEM((width, width), BF16),
            pltpu.VMEM((half * share, width), BF16),
            pltpu.SemaphoreType.DMA((steps + 2,)),
            pltpu.SemaphoreType.DMA((slots + 1,)),
        ],
        compiler_params=pltpu.CompilerParams(vmem_limit_bytes=FIRST),
        cost_estimate=pl.CostEstimate(
            flops=4 * width * width * loads, bytes_accessed=2_200_000, transcendentals=0
        ),
    )(targets, rhs_low, inv_low, blocks)


def prepared(place, rhs_low, inv_low, answer0, level):
    _, held, share, width = answer0.shape
    lanes = max(share, 128)
    per_lanes = lanes // share

    def body(place_ref, rhs_ref, inv_ref, answer0_ref, out_ref, inverse_ref, first_ref):
        turned = rhs_ref[0].astype(F32).T
        picked = turned[:share]
        for other in range(1, per_lanes):
            picked = jnp.where(
                place_ref[0] % per_lanes == other,
                turned[other * share : (other + 1) * share],
                picked,
            )
        out_ref[...] = picked.astype(BF16)
        inverse_ref[...] = inv_ref[0]
        first_ref[...] = answer0_ref[0, 0]

    return pl.pallas_call(
        body,
        out_shape=(
            jax.ShapeDtypeStruct((share, width), BF16),
            jax.ShapeDtypeStruct((width, width), BF16),
            jax.ShapeDtypeStruct((share, width), BF16),
        ),
        grid_spec=pltpu.PrefetchScalarGridSpec(
            num_scalar_prefetch=1,
            grid=(1,),
            in_specs=[
                pl.BlockSpec((1, width, lanes), lambda i, p: (level, 0, p[0] // per_lanes)),
                pl.BlockSpec((1, width, width), lambda i, p: (level, 0, 0)),
                pl.BlockSpec((1, 1, share, width), lambda i, p: (p[0] % 2, p[0] // 2, 0, 0)),
            ],
            out_specs=(
                pl.BlockSpec((share, width), lambda i, p: (0, 0)),
                pl.BlockSpec((width, width), lambda i, p: (0, 0)),
                pl.BlockSpec((share, width), lambda i, p: (0, 0)),
            ),
        ),
        compiler_params=pltpu.CompilerParams(vmem_limit_bytes=SMALL),
        cost_estimate=pl.CostEstimate(
            flops=width * width * 1000, bytes_accessed=2_000_000, transcendentals=0
        ),
    )(place, rhs_low, inv_low, answer0)


def second_level(part, right_side, inverse, first, copies):
    share, width = part.shape

    def body(part_ref, rhs_ref, inv_ref, first_ref, answer_ref, both_ref):
        residual = (rhs_ref[...].astype(F32) - part_ref[...].astype(F32)).astype(BF16)
        answer = dot_nt(residual, inv_ref[...]).astype(BF16)
        for copy in range(copies):
            answer_ref[copy] = answer
        both_ref[0] = first_ref[...]
        both_ref[1] = answer

    return pl.pallas_call(
        body,
        out_shape=(
            jax.ShapeDtypeStruct((copies, share, width), BF16),
            jax.ShapeDtypeStruct((2, share, width), BF16),
        ),
        compiler_params=pltpu.CompilerParams(vmem_limit_bytes=SMALL),
        cost_estimate=pl.CostEstimate(
            flops=2 * width * width * share, bytes_accessed=600_000, transcendentals=0
        ),
    )(part, right_side, inverse, first)


def ancestor_parts(targets, place, own, near, before=None):
    loads, width = near[0][4], near[0][1].shape[-1]
    count = near[0][5]
    terms = len(own) + len(near)

    def body(targets_ref, place_ref, *refs):
        answers, blocks, rest = refs[:terms], refs[terms : 2 * terms], refs[2 * terms :]
        total = None
        for index in range(terms):
            if index < len(own):
                _, found = slot_of(targets_ref, own[index][0], pl.program_id(0) + 2, count)
                value = answers[index][0].reshape(loads, width)
                product = dot_nt(value, blocks[index][0, 0])
                product = product * jnp.where(found == 1, 1.0, 0.0).astype(F32)
            else:
                product = dot_nt(answers[index][...], blocks[index][...])
            total = product if total is None else total + product
        if before is not None:
            total += rest[0][...].astype(F32)
        rest[-1][...] = total.astype(BF16)

    def own_answer(answer):
        return pl.BlockSpec((1, *answer.shape[1:]), lambda a, t, p: (p[1], 0, 0, 0))

    def own_block(level):
        return pl.BlockSpec(
            (1, 1, width, width),
            lambda a, t, p: (level, slot_of(t, level, a + 2, count)[0], 0, 0),
        )

    def near_answer(spot):
        return pl.BlockSpec((loads, width), lambda a, t, p: (spot, 0))

    def near_block(level):
        return pl.BlockSpec((width, width), lambda a, t, p: (level * count + a, 0))

    out_spec = pl.BlockSpec((loads, width), lambda a, t, p: (0, a))
    in_specs = [own_answer(term[2]) for term in own] + [near_answer(term[3]) for term in near]
    in_specs += [own_block(term[0]) for term in own] + [near_block(term[0]) for term in near]
    operands = [term[2] for term in (*own, *near)] + [term[1] for term in (*own, *near)]
    if before is not None:
        in_specs.append(out_spec)
        operands.append(before)
    return pl.pallas_call(
        body,
        out_shape=jax.ShapeDtypeStruct((loads, count * width), BF16),
        grid_spec=pltpu.PrefetchScalarGridSpec(
            num_scalar_prefetch=2, grid=(count,), in_specs=in_specs, out_specs=out_spec
        ),
        compiler_params=pltpu.CompilerParams(vmem_limit_bytes=LARGE),
        cost_estimate=pl.CostEstimate(
            flops=2 * terms * count * width * width * loads,
            bytes_accessed=5_000_000,
            transcendentals=0,
        ),
    )(targets, place, *operands)


def ancestor_solve(arrived, rhs_anc, inv_anc):
    sources, loads, _ = arrived.shape
    count, _, width = rhs_anc.shape

    def body(arrived_ref, rhs_ref, inv_ref, out_ref):
        total = jnp.sum(arrived_ref[...].astype(F32), axis=0)
        residual = (rhs_ref[0].astype(F32) - total).astype(BF16)
        out_ref[0] = dot_nt(residual, inv_ref[0])

    return pl.pallas_call(
        body,
        out_shape=jax.ShapeDtypeStruct((count, loads, width), F32),
        grid=(count,),
        in_specs=[
            pl.BlockSpec((sources, loads, width), lambda a: (0, 0, a)),
            pl.BlockSpec((1, loads, width), lambda a: (a, 0, 0)),
            pl.BlockSpec((1, width, width), lambda a: (a, 0, 0)),
        ],
        out_specs=pl.BlockSpec((1, loads, width), lambda a: (a, 0, 0)),
        compiler_params=pltpu.CompilerParams(vmem_limit_bytes=LARGE),
        cost_estimate=pl.CostEstimate(
            flops=2 * count * width * width * loads, bytes_accessed=3_000_000, transcendentals=0
        ),
    )(arrived, rhs_anc, inv_anc)


def on_device(rhs_low, inv_low, blocks, targets, rhs_anc, inv_anc):
    rows, cols = lax.axis_size("row"), lax.axis_size("col")
    rhs_low, inv_low = rhs_low[0, :, 0], inv_low[0, :, 0]
    blocks, targets = blocks[0, 0, 0], targets[0, 0, 0]
    width, loads = rhs_low.shape[1:]
    layers = lax.axis_size("layer")
    place = jnp.stack([lax.axis_index("row"), lax.axis_index("layer") & 1]).astype(jnp.int32)

    answer0, part, give = first_level(targets, rhs_low, inv_low, blocks, rows)
    ready = prepared(place, rhs_low, inv_low, answer0, 1)
    shares = lax.all_to_all(part, "col", 0, 0, tiled=True)

    def neighbour(layer, row):
        ahead = (layer + row) % 2 == 0
        return (layer + (1 if ahead else -1)) % layers

    pairs = [
        (layer * rows + row, neighbour(layer, row) * rows + row)
        for layer in range(layers)
        for row in range(rows)
    ]

    def swap(value):
        return lax.ppermute(value, ("layer", "row"), pairs)

    near = swap(give)

    summed = shares.astype(F32).sum(axis=0).astype(BF16)
    turn = [
        (row * cols + col, col * cols + (row - 1) % rows)
        for row in range(rows)
        for col in range(cols)
    ]
    summed = lax.ppermute(summed, ("row", "col"), turn)
    pieces, both = second_level(summed, *ready, rows // 2)
    lines = [list(range(core, rows, 2)) for core in range(2)]
    chips = [[row, row + 1] for row in range(0, rows, 2)]
    pieces = lax.all_to_all(pieces, "row", 0, 0, axis_index_groups=lines, tiled=True)
    answer1 = lax.all_gather(pieces, "row", axis=0, axis_index_groups=chips)

    near_answer1 = swap(lax.dynamic_index_in_dim(answer1, 1 - place[1], 0, keepdims=False))
    wanted, count = loads // 2, inv_anc.shape[0]
    near_answer1 = near_answer1.reshape(wanted, width)
    own = [(0, blocks, answer0), (1, blocks, answer1)]
    early = (0, near, near, near.shape[0] // wanted - 1, wanted, count)
    late = (1, near, near_answer1, 0, wanted, count)
    parts = ancestor_parts(targets, place, own, [early])
    parts = ancestor_parts(targets, place, [], [late], parts)
    groups = [
        [layer * cols + col for layer in range(parity, layers, 2) for col in range(cols)]
        for parity in range(2)
    ]
    members = len(groups[0])
    arrived = lax.all_to_all(
        parts.reshape(members, parts.shape[0] // members, -1),
        ("layer", "col"),
        0,
        0,
        axis_index_groups=groups,
        tiled=True,
    )
    solved = ancestor_solve(arrived, jnp.swapaxes(rhs_anc, 1, 2), inv_anc)
    return (jnp.swapaxes(both, 1, 2)[None, :, None], jnp.swapaxes(solved, 1, 2))


def solution(mesh):
    in_specs = (
        P("layer", None, "col", None, None),
        P("layer", None, "col", None, None),
        P("layer", "row", "col", None, None, None, None),
        P("layer", "row", "col", None, None),
        P("row", None, ("layer", "col")),
        P("row", None, None),
    )
    out_specs = (P("layer", None, "col", None, "row"), P("row", None, ("layer", "col")))
    return jax.shard_map(
        on_device, mesh=mesh, in_specs=in_specs, out_specs=out_specs, check_vma=False
    )
```

```python
import jax
import jax.numpy as jnp
from jax import lax
from jax.experimental import pallas as pl
from jax.experimental.pallas import tpu as pltpu
from jax.sharding import PartitionSpec as P

F32 = jnp.float32
BF16 = jnp.bfloat16
SMALL = 8 << 20
LARGE = 24 << 20
FIRST = 60 << 20
NT = (((1,), (1,)), ((), ()))


def dot_nt(left, right):
    return lax.dot_general(left, right, NT, preferred_element_type=F32)


def slot_of(targets_ref, level, target, per_row):
    slot, found = jnp.int32(0), jnp.int32(0)
    for member in range(per_row):
        hit = targets_ref[level, member] == target
        slot = jnp.where(hit, jnp.int32(member), slot)
        found = jnp.where(hit, jnp.int32(1), found)
    return slot, found


def first_level(targets, rhs_low, inv_low, blocks, rows):
    levels, width, loads = rhs_low.shape
    per_row = blocks.shape[1]
    share = loads // rows
    steps = 2
    held, half = rows // steps, rows // 2
    slots = levels * per_row

    def body(
        targets_ref, rhs_ref, inv_ref, blocks_ref, answer_ref, part_ref, give_ref,
        rhs_in, inv_in, blocks_in, zeros, half_out, in_sems, blocks_sems, out_sems,
    ):
        kept = lax.axis_index("layer") % 2
        inv_copy = pltpu.make_async_copy(inv_ref.at[0], inv_in, in_sems.at[steps])
        rhs_copies = [
            pltpu.make_async_copy(
                rhs_ref.at[0, :, pl.ds(step * (loads // steps), loads // steps)],
                rhs_in.at[step],
                in_sems.at[step],
            )
            for step in range(steps)
        ]
        blocks_copies = [
            pltpu.make_async_copy(
                blocks_ref.at[index // per_row, index % per_row],
                blocks_in.at[index // per_row, index % per_row],
                blocks_sems.at[index],
            )
            for index in range(slots)
        ]
        for copy in (inv_copy, *rhs_copies, *blocks_copies):
            copy.start()
        zeros[...] = jnp.zeros_like(zeros)
        inv_copy.wait()
        answers = []
        for step in range(steps):
            rhs_copies[step].wait()
            answer = jnp.dot(inv_in[...], rhs_in[step], preferred_element_type=F32).T.astype(BF16)
            answers.append(answer)
            pieces = [answer[member * share : (member + 1) * share] for member in range(held)]
            for member in range(held):
                answer_ref[member % 2, step * (held // 2) + member // 2] = pieces[member]
            for member in range(0, held, 2):
                start = (step * (held // 2) + member // 2) * share

                @pl.when(kept == 1)
                def _(start=start, piece=pieces[member]):
                    half_out[start : start + share] = piece

                @pl.when(kept == 0)
                def _(start=start, piece=pieces[member + 1]):
                    half_out[start : start + share] = piece

        half_copy = pltpu.make_async_copy(
            half_out, give_ref.at[pl.ds(slots * width, half * share)], out_sems.at[slots]
        )
        half_copy.start()
        for copy in blocks_copies:
            copy.wait()

        def give(index):
            return give_ref.at[pl.ds(index * width, width)]

        for index in range(slots):
            level, ancestor = index // per_row, index % per_row
            source, named = slot_of(targets_ref, level, ancestor + 2, per_row)

            @pl.when(named == 1)
            def _(index=index, level=level, source=source):
                pltpu.make_async_copy(
                    blocks_in.at[level, source], give(index), out_sems.at[index]
                ).start()

            @pl.when(named == 0)
            def _(index=index):
                pltpu.make_async_copy(zeros, give(index), out_sems.at[index]).start()

        slot, found = slot_of(targets_ref, 0, 1, per_row)

        @pl.when(found == 1)
        def _():
            for step in range(steps):
                part = dot_nt(answers[step], blocks_in[0, slot]).astype(BF16)
                part_ref[step * held : (step + 1) * held] = part.reshape(held, share, width)

        @pl.when(found == 0)
        def _():
            part_ref[...] = jnp.zeros_like(part_ref)

        for index in range(slots):
            pltpu.make_async_copy(zeros, give(index), out_sems.at[index]).wait()
        half_copy.wait()

    any_spec, vmem = pl.BlockSpec(memory_space=pl.ANY), pl.BlockSpec(memory_space=pltpu.VMEM)
    return pl.pallas_call(
        body,
        out_shape=(
            jax.ShapeDtypeStruct((2, half, share, width), BF16),
            jax.ShapeDtypeStruct((rows, share, width), BF16),
            jax.ShapeDtypeStruct((slots * width + half * share, width), BF16),
        ),
        in_specs=[pl.BlockSpec(memory_space=pltpu.SMEM), any_spec, any_spec, any_spec],
        out_specs=(vmem, vmem, any_spec),
        scratch_shapes=[
            pltpu.VMEM((steps, width, loads // steps), BF16),
            pltpu.VMEM((width, width), BF16),
            pltpu.VMEM(blocks.shape, BF16),
            pltpu.VMEM((width, width), BF16),
            pltpu.VMEM((half * share, width), BF16),
            pltpu.SemaphoreType.DMA((steps + 1,)),
            pltpu.SemaphoreType.DMA((slots,)),
            pltpu.SemaphoreType.DMA((slots + 1,)),
        ],
        compiler_params=pltpu.CompilerParams(vmem_limit_bytes=FIRST),
        cost_estimate=pl.CostEstimate(
            flops=4 * width * width * loads, bytes_accessed=2_200_000, transcendentals=0
        ),
    )(targets, rhs_low, inv_low, blocks)


def prepared(place, rhs_low, inv_low, answer0, level):
    _, held, share, width = answer0.shape
    lanes = max(share, 128)
    per_lanes = lanes // share

    def body(place_ref, rhs_ref, inv_ref, answer0_ref, out_ref, inverse_ref, first_ref):
        turned = rhs_ref[0].astype(F32).T
        picked = turned[:share]
        for other in range(1, per_lanes):
            picked = jnp.where(
                place_ref[0] % per_lanes == other,
                turned[other * share : (other + 1) * share],
                picked,
            )
        out_ref[...] = picked.astype(BF16)
        inverse_ref[...] = inv_ref[0]
        first_ref[...] = answer0_ref[0, 0]

    return pl.pallas_call(
        body,
        out_shape=(
            jax.ShapeDtypeStruct((share, width), BF16),
            jax.ShapeDtypeStruct((width, width), BF16),
            jax.ShapeDtypeStruct((share, width), BF16),
        ),
        grid_spec=pltpu.PrefetchScalarGridSpec(
            num_scalar_prefetch=1,
            grid=(1,),
            in_specs=[
                pl.BlockSpec((1, width, lanes), lambda i, p: (level, 0, p[0] // per_lanes)),
                pl.BlockSpec((1, width, width), lambda i, p: (level, 0, 0)),
                pl.BlockSpec((1, 1, share, width), lambda i, p: (p[0] % 2, p[0] // 2, 0, 0)),
            ],
            out_specs=(
                pl.BlockSpec((share, width), lambda i, p: (0, 0)),
                pl.BlockSpec((width, width), lambda i, p: (0, 0)),
                pl.BlockSpec((share, width), lambda i, p: (0, 0)),
            ),
        ),
        compiler_params=pltpu.CompilerParams(vmem_limit_bytes=SMALL),
        cost_estimate=pl.CostEstimate(
            flops=width * width * 1000, bytes_accessed=2_000_000, transcendentals=0
        ),
    )(place, rhs_low, inv_low, answer0)


def second_level(part, right_side, inverse, first, copies):
    share, width = part.shape

    def body(part_ref, rhs_ref, inv_ref, first_ref, answer_ref, both_ref):
        residual = (rhs_ref[...].astype(F32) - part_ref[...].astype(F32)).astype(BF16)
        answer = dot_nt(residual, inv_ref[...]).astype(BF16)
        for copy in range(copies):
            answer_ref[copy] = answer
        both_ref[0] = first_ref[...]
        both_ref[1] = answer

    return pl.pallas_call(
        body,
        out_shape=(
            jax.ShapeDtypeStruct((copies, share, width), BF16),
            jax.ShapeDtypeStruct((2, share, width), BF16),
        ),
        compiler_params=pltpu.CompilerParams(vmem_limit_bytes=SMALL),
        cost_estimate=pl.CostEstimate(
            flops=2 * width * width * share, bytes_accessed=600_000, transcendentals=0
        ),
    )(part, right_side, inverse, first)


def ancestor_parts(targets, place, own, near, before=None):
    loads, width = near[0][4], near[0][1].shape[-1]
    count = near[0][5]
    terms = len(own) + len(near)

    def body(targets_ref, place_ref, *refs):
        answers, blocks, rest = refs[:terms], refs[terms : 2 * terms], refs[2 * terms :]
        total = None
        for index in range(terms):
            if index < len(own):
                _, found = slot_of(targets_ref, own[index][0], pl.program_id(0) + 2, count)
                value = answers[index][0].reshape(loads, width)
                product = dot_nt(value, blocks[index][0, 0])
                product = product * jnp.where(found == 1, 1.0, 0.0).astype(F32)
            else:
                product = dot_nt(answers[index][...], blocks[index][...])
            total = product if total is None else total + product
        if before is not None:
            total += rest[0][...].astype(F32)
        rest[-1][...] = total.astype(BF16)

    def own_answer(answer):
        return pl.BlockSpec((1, *answer.shape[1:]), lambda a, t, p: (p[1], 0, 0, 0))

    def own_block(level):
        return pl.BlockSpec(
            (1, 1, width, width),
            lambda a, t, p: (level, slot_of(t, level, a + 2, count)[0], 0, 0),
        )

    def near_answer(spot):
        return pl.BlockSpec((loads, width), lambda a, t, p: (spot, 0))

    def near_block(level):
        return pl.BlockSpec((width, width), lambda a, t, p: (level * count + a, 0))

    out_spec = pl.BlockSpec((loads, width), lambda a, t, p: (0, a))
    in_specs = [own_answer(term[2]) for term in own] + [near_answer(term[3]) for term in near]
    in_specs += [own_block(term[0]) for term in own] + [near_block(term[0]) for term in near]
    operands = [term[2] for term in (*own, *near)] + [term[1] for term in (*own, *near)]
    if before is not None:
        in_specs.append(out_spec)
        operands.append(before)
    return pl.pallas_call(
        body,
        out_shape=jax.ShapeDtypeStruct((loads, count * width), BF16),
        grid_spec=pltpu.PrefetchScalarGridSpec(
            num_scalar_prefetch=2, grid=(count,), in_specs=in_specs, out_specs=out_spec
        ),
        compiler_params=pltpu.CompilerParams(vmem_limit_bytes=LARGE),
        cost_estimate=pl.CostEstimate(
            flops=2 * terms * count * width * width * loads,
            bytes_accessed=5_000_000,
            transcendentals=0,
        ),
    )(targets, place, *operands)


def ancestor_solve(arrived, rhs_anc, inv_anc):
    sources, loads, _ = arrived.shape
    count, _, width = rhs_anc.shape

    def body(arrived_ref, rhs_ref, inv_ref, out_ref):
        total = jnp.sum(arrived_ref[...].astype(F32), axis=0)
        residual = (rhs_ref[0].astype(F32) - total).astype(BF16)
        out_ref[0] = dot_nt(residual, inv_ref[0])

    return pl.pallas_call(
        body,
        out_shape=jax.ShapeDtypeStruct((count, loads, width), F32),
        grid=(count,),
        in_specs=[
            pl.BlockSpec((sources, loads, width), lambda a: (0, 0, a)),
            pl.BlockSpec((1, loads, width), lambda a: (a, 0, 0)),
            pl.BlockSpec((1, width, width), lambda a: (a, 0, 0)),
        ],
        out_specs=pl.BlockSpec((1, loads, width), lambda a: (a, 0, 0)),
        compiler_params=pltpu.CompilerParams(vmem_limit_bytes=LARGE),
        cost_estimate=pl.CostEstimate(
            flops=2 * count * width * width * loads, bytes_accessed=3_000_000, transcendentals=0
        ),
    )(arrived, rhs_anc, inv_anc)


def on_device(rhs_low, inv_low, blocks, targets, rhs_anc, inv_anc):
    rows, cols = lax.axis_size("row"), lax.axis_size("col")
    rhs_low, inv_low = rhs_low[0, :, 0], inv_low[0, :, 0]
    blocks, targets = blocks[0, 0, 0], targets[0, 0, 0]
    width, loads = rhs_low.shape[1:]
    layers = lax.axis_size("layer")
    place = jnp.stack([lax.axis_index("row"), lax.axis_index("layer") & 1]).astype(jnp.int32)

    answer0, part, give = first_level(targets, rhs_low, inv_low, blocks, rows)
    ready = prepared(place, rhs_low, inv_low, answer0, 1)
    shares = lax.all_to_all(part, "col", 0, 0, tiled=True)

    def neighbour(layer, row):
        ahead = (layer + row) % 2 == 0
        return (layer + (1 if ahead else -1)) % layers

    pairs = [
        (layer * rows + row, neighbour(layer, row) * rows + row)
        for layer in range(layers)
        for row in range(rows)
    ]

    def swap(value):
        return lax.ppermute(value, ("layer", "row"), pairs)

    near = swap(give)

    summed = shares.astype(F32).sum(axis=0).astype(BF16)
    turn = [
        (row * cols + col, col * cols + (row - 1) % rows)
        for row in range(rows)
        for col in range(cols)
    ]
    summed = lax.ppermute(summed, ("row", "col"), turn)
    pieces, both = second_level(summed, *ready, rows // 2)
    lines = [list(range(core, rows, 2)) for core in range(2)]
    chips = [[row, row + 1] for row in range(0, rows, 2)]
    pieces = lax.all_to_all(pieces, "row", 0, 0, axis_index_groups=lines, tiled=True)
    answer1 = lax.all_gather(pieces, "row", axis=0, axis_index_groups=chips)

    near_answer1 = swap(lax.dynamic_index_in_dim(answer1, 1 - place[1], 0, keepdims=False))
    wanted, count = loads // 2, inv_anc.shape[0]
    near_answer1 = near_answer1.reshape(wanted, width)
    own = [(0, blocks, answer0), (1, blocks, answer1)]
    early = (0, near, near, near.shape[0] // wanted - 1, wanted, count)
    late = (1, near, near_answer1, 0, wanted, count)
    parts = ancestor_parts(targets, place, own, [early])
    parts = ancestor_parts(targets, place, [], [late], parts)
    groups = [
        [layer * cols + col for layer in range(parity, layers, 2) for col in range(cols)]
        for parity in range(2)
    ]
    members = len(groups[0])
    arrived = lax.all_to_all(
        parts.reshape(members, parts.shape[0] // members, -1),
        ("layer", "col"),
        0,
        0,
        axis_index_groups=groups,
        tiled=True,
    )
    solved = ancestor_solve(arrived, jnp.swapaxes(rhs_anc, 1, 2), inv_anc)
    return (jnp.swapaxes(both, 1, 2)[None, :, None], jnp.swapaxes(solved, 1, 2))


def solution(mesh):
    in_specs = (
        P("layer", None, "col", None, None),
        P("layer", None, "col", None, None),
        P("layer", "row", "col", None, None, None, None),
        P("layer", "row", "col", None, None),
        P("row", None, ("layer", "col")),
        P("row", None, None),
    )
    out_specs = (P("layer", None, "col", None, "row"), P("row", None, ("layer", "col")))
    return jax.shard_map(
        on_device, mesh=mesh, in_specs=in_specs, out_specs=out_specs, check_vma=False
    )
```

```python
import jax
import jax.numpy as jnp
from jax import lax
from jax.experimental import pallas as pl
from jax.experimental.pallas import tpu as pltpu
from jax.sharding import PartitionSpec as P

F32 = jnp.float32
BF16 = jnp.bfloat16
SMALL = 8 << 20
LARGE = 24 << 20
FIRST = 58 << 20
NT = (((1,), (1,)), ((), ()))


def dot_nt(left, right):
    return lax.dot_general(left, right, NT, preferred_element_type=F32)


def slot_of(targets_ref, level, target, per_row):
    slot, found = jnp.int32(0), jnp.int32(0)
    for member in range(per_row):
        hit = targets_ref[level, member] == target
        slot = jnp.where(hit, jnp.int32(member), slot)
        found = jnp.where(hit, jnp.int32(1), found)
    return slot, found


def first_level(targets, rhs_low, inv_low, blocks, rows):
    levels, width, loads = rhs_low.shape
    per_row = blocks.shape[1]
    share = loads // rows
    steps = 2
    held, half = rows // steps, rows // 2
    slots = levels * per_row

    def body(
        targets_ref, rhs_ref, inv_ref, blocks_ref, answer_ref, part_ref, give_ref,
        rhs_in, inv_in, blocks_in, zeros, half_out, in_sems, blocks_sems, out_sems,
    ):
        kept = lax.axis_index("layer") % 2
        inv_copy = pltpu.make_async_copy(inv_ref.at[0], inv_in, in_sems.at[steps])
        rhs_copies = [
            pltpu.make_async_copy(
                rhs_ref.at[0, :, pl.ds(step * (loads // steps), loads // steps)],
                rhs_in.at[step],
                in_sems.at[step],
            )
            for step in range(steps)
        ]
        blocks_copies = [
            pltpu.make_async_copy(blocks_ref.at[level], blocks_in.at[level], blocks_sems.at[level])
            for level in range(levels)
        ]

        def give(index):
            return give_ref.at[pl.ds(index * width, width)]

        def pass_on(level):
            blocks_copies[level].wait()
            for ancestor in range(per_row):
                index = level * per_row + ancestor
                source, named = slot_of(targets_ref, level, ancestor + 2, per_row)

                @pl.when(named == 1)
                def _(index=index, source=source):
                    pltpu.make_async_copy(
                        blocks_in.at[level, source], give(index), out_sems.at[index]
                    ).start()

                @pl.when(named == 0)
                def _(index=index):
                    pltpu.make_async_copy(zeros, give(index), out_sems.at[index]).start()

        for copy in (inv_copy, *rhs_copies, *blocks_copies):
            copy.start()
        zeros[...] = jnp.zeros_like(zeros)
        inv_copy.wait()
        answers = []
        for step in range(steps):
            if step > 0:
                pass_on(step - 1)
            rhs_copies[step].wait()
            answer = jnp.dot(inv_in[...], rhs_in[step], preferred_element_type=F32).T.astype(BF16)
            answers.append(answer)
            pieces = [answer[member * share : (member + 1) * share] for member in range(held)]
            for member in range(held):
                answer_ref[member % 2, step * (held // 2) + member // 2] = pieces[member]
            for member in range(0, held, 2):
                start = (step * (held // 2) + member // 2) * share

                @pl.when(kept == 1)
                def _(start=start, piece=pieces[member]):
                    half_out[start : start + share] = piece

                @pl.when(kept == 0)
                def _(start=start, piece=pieces[member + 1]):
                    half_out[start : start + share] = piece

        half_copy = pltpu.make_async_copy(
            half_out, give_ref.at[pl.ds(slots * width, half * share)], out_sems.at[slots]
        )
        half_copy.start()
        for level in range(steps - 1, levels):
            pass_on(level)
        slot, found = slot_of(targets_ref, 0, 1, per_row)

        @pl.when(found == 1)
        def _():
            for step in range(steps):
                part = dot_nt(answers[step], blocks_in[0, slot]).astype(BF16)
                part_ref[step * held : (step + 1) * held] = part.reshape(held, share, width)

        @pl.when(found == 0)
        def _():
            part_ref[...] = jnp.zeros_like(part_ref)

        for index in range(slots):
            pltpu.make_async_copy(zeros, give(index), out_sems.at[index]).wait()
        half_copy.wait()

    any_spec, vmem = pl.BlockSpec(memory_space=pl.ANY), pl.BlockSpec(memory_space=pltpu.VMEM)
    return pl.pallas_call(
        body,
        out_shape=(
            jax.ShapeDtypeStruct((2, half, share, width), BF16),
            jax.ShapeDtypeStruct((rows, share, width), BF16),
            jax.ShapeDtypeStruct((slots * width + half * share, width), BF16),
        ),
        in_specs=[pl.BlockSpec(memory_space=pltpu.SMEM), any_spec, any_spec, any_spec],
        out_specs=(vmem, vmem, any_spec),
        scratch_shapes=[
            pltpu.VMEM((steps, width, loads // steps), BF16),
            pltpu.VMEM((width, width), BF16),
            pltpu.VMEM(blocks.shape, BF16),
            pltpu.VMEM((width, width), BF16),
            pltpu.VMEM((half * share, width), BF16),
            pltpu.SemaphoreType.DMA((steps + 1,)),
            pltpu.SemaphoreType.DMA((levels,)),
            pltpu.SemaphoreType.DMA((slots + 1,)),
        ],
        compiler_params=pltpu.CompilerParams(vmem_limit_bytes=FIRST),
        cost_estimate=pl.CostEstimate(
            flops=4 * width * width * loads, bytes_accessed=2_200_000, transcendentals=0
        ),
    )(targets, rhs_low, inv_low, blocks)


def prepared(place, rhs_low, inv_low, answer0, level):
    _, held, share, width = answer0.shape
    lanes = max(share, 128)
    per_lanes = lanes // share

    def body(place_ref, rhs_ref, inv_ref, answer0_ref, out_ref, inverse_ref, first_ref):
        turned = rhs_ref[0].astype(F32).T
        picked = turned[:share]
        for other in range(1, per_lanes):
            picked = jnp.where(
                place_ref[0] % per_lanes == other,
                turned[other * share : (other + 1) * share],
                picked,
            )
        out_ref[...] = picked.astype(BF16)
        inverse_ref[...] = inv_ref[0]
        first_ref[...] = answer0_ref[0, 0]

    return pl.pallas_call(
        body,
        out_shape=(
            jax.ShapeDtypeStruct((share, width), BF16),
            jax.ShapeDtypeStruct((width, width), BF16),
            jax.ShapeDtypeStruct((share, width), BF16),
        ),
        grid_spec=pltpu.PrefetchScalarGridSpec(
            num_scalar_prefetch=1,
            grid=(1,),
            in_specs=[
                pl.BlockSpec((1, width, lanes), lambda i, p: (level, 0, p[0] // per_lanes)),
                pl.BlockSpec((1, width, width), lambda i, p: (level, 0, 0)),
                pl.BlockSpec((1, 1, share, width), lambda i, p: (p[0] % 2, p[0] // 2, 0, 0)),
            ],
            out_specs=(
                pl.BlockSpec((share, width), lambda i, p: (0, 0)),
                pl.BlockSpec((width, width), lambda i, p: (0, 0)),
                pl.BlockSpec((share, width), lambda i, p: (0, 0)),
            ),
        ),
        compiler_params=pltpu.CompilerParams(vmem_limit_bytes=SMALL),
        cost_estimate=pl.CostEstimate(
            flops=width * width * 1000, bytes_accessed=2_000_000, transcendentals=0
        ),
    )(place, rhs_low, inv_low, answer0)


def second_level(part, right_side, inverse, first, copies):
    share, width = part.shape

    def body(part_ref, rhs_ref, inv_ref, first_ref, answer_ref, both_ref):
        residual = (rhs_ref[...].astype(F32) - part_ref[...].astype(F32)).astype(BF16)
        answer = dot_nt(residual, inv_ref[...]).astype(BF16)
        for copy in range(copies):
            answer_ref[copy] = answer
        both_ref[0] = first_ref[...]
        both_ref[1] = answer

    return pl.pallas_call(
        body,
        out_shape=(
            jax.ShapeDtypeStruct((copies, share, width), BF16),
            jax.ShapeDtypeStruct((2, share, width), BF16),
        ),
        compiler_params=pltpu.CompilerParams(vmem_limit_bytes=SMALL),
        cost_estimate=pl.CostEstimate(
            flops=2 * width * width * share, bytes_accessed=600_000, transcendentals=0
        ),
    )(part, right_side, inverse, first)


def ancestor_parts(place, own, near, room, before=None):
    loads, width, count = near[0][4], near[0][1].shape[-1], near[0][5]
    terms = len(own) + len(near)

    def body(place_ref, *refs):
        answers, blocks, rest = refs[:terms], refs[terms : 2 * terms], refs[2 * terms :]
        total = None
        for index in range(terms):
            value = answers[index]
            value = value[0].reshape(loads, width) if index < len(own) else value[...]
            product = dot_nt(value, blocks[index][...])
            total = product if total is None else total + product
        if before is not None:
            total += rest[0][...].astype(F32)
        rest[-1][...] = total.astype(BF16)

    def own_answer(answer):
        return pl.BlockSpec((1, *answer.shape[1:]), lambda a, p: (p[1], 0, 0, 0))

    def near_answer(spot):
        return pl.BlockSpec((loads, width), lambda a, p: (spot, 0))

    def block(level):
        return pl.BlockSpec((width, width), lambda a, p: (level * count + a, 0))

    out_spec = pl.BlockSpec((loads, width), lambda a, p: (0, a))
    in_specs = [own_answer(term[2]) for term in own] + [near_answer(term[3]) for term in near]
    in_specs += [block(term[0]) for term in (*own, *near)]
    operands = [term[2] for term in (*own, *near)] + [term[1] for term in (*own, *near)]
    if before is not None:
        in_specs.append(out_spec)
        operands.append(before)
    return pl.pallas_call(
        body,
        out_shape=jax.ShapeDtypeStruct((loads, count * width), BF16),
        grid_spec=pltpu.PrefetchScalarGridSpec(
            num_scalar_prefetch=1, grid=(count,), in_specs=in_specs, out_specs=out_spec
        ),
        compiler_params=pltpu.CompilerParams(vmem_limit_bytes=room),
        cost_estimate=pl.CostEstimate(
            flops=2 * terms * count * width * width * loads,
            bytes_accessed=5_000_000,
            transcendentals=0,
        ),
    )(place, *operands)


def ancestor_solve(arrived, rhs_anc, inv_anc):
    sources, loads, _ = arrived.shape
    count, _, width = rhs_anc.shape

    def body(arrived_ref, rhs_ref, inv_ref, out_ref):
        total = jnp.sum(arrived_ref[...].astype(F32), axis=0)
        residual = (rhs_ref[0].astype(F32) - total).astype(BF16)
        out_ref[0] = dot_nt(residual, inv_ref[0])

    return pl.pallas_call(
        body,
        out_shape=jax.ShapeDtypeStruct((count, loads, width), F32),
        grid=(count,),
        in_specs=[
            pl.BlockSpec((sources, loads, width), lambda a: (0, 0, a)),
            pl.BlockSpec((1, loads, width), lambda a: (a, 0, 0)),
            pl.BlockSpec((1, width, width), lambda a: (a, 0, 0)),
        ],
        out_specs=pl.BlockSpec((1, loads, width), lambda a: (a, 0, 0)),
        compiler_params=pltpu.CompilerParams(vmem_limit_bytes=LARGE),
        cost_estimate=pl.CostEstimate(
            flops=2 * count * width * width * loads, bytes_accessed=3_000_000, transcendentals=0
        ),
    )(arrived, rhs_anc, inv_anc)


def on_device(rhs_low, inv_low, blocks, targets, rhs_anc, inv_anc):
    rows, cols = lax.axis_size("row"), lax.axis_size("col")
    rhs_low, inv_low = rhs_low[0, :, 0], inv_low[0, :, 0]
    blocks, targets = blocks[0, 0, 0], targets[0, 0, 0]
    width, loads = rhs_low.shape[1:]
    layers = lax.axis_size("layer")
    place = jnp.stack([lax.axis_index("row"), lax.axis_index("layer") & 1]).astype(jnp.int32)

    answer0, part, give = first_level(targets, rhs_low, inv_low, blocks, rows)
    ready = prepared(place, rhs_low, inv_low, answer0, 1)
    shares = lax.all_to_all(part, "col", 0, 0, tiled=True)

    def neighbour(layer, row):
        ahead = (layer + row) % 2 == 0
        return (layer + (1 if ahead else -1)) % layers

    pairs = [
        (layer * rows + row, neighbour(layer, row) * rows + row)
        for layer in range(layers)
        for row in range(rows)
    ]

    def swap(value):
        return lax.ppermute(value, ("layer", "row"), pairs)

    near = swap(give)

    summed = shares.astype(F32).sum(axis=0).astype(BF16)
    turn = [
        (row * cols + col, col * cols + (row - 1) % rows)
        for row in range(rows)
        for col in range(cols)
    ]
    summed = lax.ppermute(summed, ("row", "col"), turn)
    pieces, both = second_level(summed, *ready, rows // 2)
    lines = [list(range(core, rows, 2)) for core in range(2)]
    chips = [[row, row + 1] for row in range(0, rows, 2)]
    pieces = lax.all_to_all(pieces, "row", 0, 0, axis_index_groups=lines, tiled=True)
    answer1 = lax.all_gather(pieces, "row", axis=0, axis_index_groups=chips)

    near_answer1 = swap(lax.dynamic_index_in_dim(answer1, 1 - place[1], 0, keepdims=False))
    wanted, count = loads // 2, inv_anc.shape[0]
    near_answer1 = near_answer1.reshape(wanted, width)
    own = [(0, give, answer0), (1, give, answer1)]
    early = (0, near, near, near.shape[0] // wanted - 1, wanted, count)
    late = (1, near, near_answer1, 0, wanted, count)
    parts = ancestor_parts(place, own, [early], FIRST)
    parts = ancestor_parts(place, [], [late], FIRST, parts)
    groups = [
        [layer * cols + col for layer in range(parity, layers, 2) for col in range(cols)]
        for parity in range(2)
    ]
    members = len(groups[0])
    arrived = lax.all_to_all(
        parts.reshape(members, parts.shape[0] // members, -1),
        ("layer", "col"),
        0,
        0,
        axis_index_groups=groups,
        tiled=True,
    )
    solved = ancestor_solve(arrived, jnp.swapaxes(rhs_anc, 1, 2), inv_anc)
    return (jnp.swapaxes(both, 1, 2)[None, :, None], jnp.swapaxes(solved, 1, 2))


def solution(mesh):
    in_specs = (
        P("layer", None, "col", None, None),
        P("layer", None, "col", None, None),
        P("layer", "row", "col", None, None, None, None),
        P("layer", "row", "col", None, None),
        P("row", None, ("layer", "col")),
        P("row", None, None),
    )
    out_specs = (P("layer", None, "col", None, "row"), P("row", None, ("layer", "col")))
    return jax.shard_map(
        on_device, mesh=mesh, in_specs=in_specs, out_specs=out_specs, check_vma=False
    )
```

```python
import jax
import jax.numpy as jnp
from jax import lax
from jax.experimental import pallas as pl
from jax.experimental.pallas import tpu as pltpu
from jax.sharding import PartitionSpec as P

F32 = jnp.float32
BF16 = jnp.bfloat16
SMALL = 8 << 20
LARGE = 24 << 20
FIRST = 60 << 20
NT = (((1,), (1,)), ((), ()))


def dot_nt(left, right):
    return lax.dot_general(left, right, NT, preferred_element_type=F32)


def slot_of(targets_ref, level, target, per_row):
    slot, found = jnp.int32(0), jnp.int32(0)
    for member in range(per_row):
        hit = targets_ref[level, member] == target
        slot = jnp.where(hit, jnp.int32(member), slot)
        found = jnp.where(hit, jnp.int32(1), found)
    return slot, found


def first_level(targets, rhs_low, inv_low, blocks, rows):
    levels, width, loads = rhs_low.shape
    per_row = blocks.shape[1]
    share = loads // rows
    steps = 2
    held, half = rows // steps, rows // 2
    slots = levels * per_row

    def body(
        targets_ref, rhs_ref, inv_ref, blocks_ref, answer_ref, part_ref, give_ref,
        rhs_in, inv_in, blocks_in, zeros, half_out, in_sems, blocks_sems, out_sems,
    ):
        kept = lax.axis_index("layer") % 2
        inv_copy = pltpu.make_async_copy(inv_ref.at[0], inv_in, in_sems.at[steps])
        rhs_copies = [
            pltpu.make_async_copy(
                rhs_ref.at[0, :, pl.ds(step * (loads // steps), loads // steps)],
                rhs_in.at[step],
                in_sems.at[step],
            )
            for step in range(steps)
        ]
        blocks_copies = [
            pltpu.make_async_copy(blocks_ref.at[level], blocks_in.at[level], blocks_sems.at[level])
            for level in range(levels)
        ]

        def give(index):
            return give_ref.at[pl.ds(index * width, width)]

        def pass_on(level):
            blocks_copies[level].wait()
            for ancestor in range(per_row):
                index = level * per_row + ancestor
                source, named = slot_of(targets_ref, level, ancestor + 2, per_row)

                @pl.when(named == 1)
                def _(index=index, source=source):
                    pltpu.make_async_copy(
                        blocks_in.at[level, source], give(index), out_sems.at[index]
                    ).start()

                @pl.when(named == 0)
                def _(index=index):
                    pltpu.make_async_copy(zeros, give(index), out_sems.at[index]).start()

        for copy in (inv_copy, *rhs_copies, *blocks_copies):
            copy.start()
        zeros[...] = jnp.zeros_like(zeros)
        inv_copy.wait()
        answers = []
        for step in range(steps):
            if step > 0:
                pass_on(step - 1)
            rhs_copies[step].wait()
            answer = jnp.dot(inv_in[...], rhs_in[step], preferred_element_type=F32).T.astype(BF16)
            answers.append(answer)
            pieces = [answer[member * share : (member + 1) * share] for member in range(held)]
            for member in range(held):
                answer_ref[member % 2, step * (held // 2) + member // 2] = pieces[member]
            for member in range(0, held, 2):
                start = (step * (held // 2) + member // 2) * share

                @pl.when(kept == 1)
                def _(start=start, piece=pieces[member]):
                    half_out[start : start + share] = piece

                @pl.when(kept == 0)
                def _(start=start, piece=pieces[member + 1]):
                    half_out[start : start + share] = piece

        half_copy = pltpu.make_async_copy(
            half_out, give_ref.at[pl.ds(slots * width, half * share)], out_sems.at[slots]
        )
        half_copy.start()
        for level in range(steps - 1, levels):
            pass_on(level)
        slot, found = slot_of(targets_ref, 0, 1, per_row)

        @pl.when(found == 1)
        def _():
            for step in range(steps):
                part = dot_nt(answers[step], blocks_in[0, slot]).astype(BF16)
                part_ref[step * held : (step + 1) * held] = part.reshape(held, share, width)

        @pl.when(found == 0)
        def _():
            part_ref[...] = jnp.zeros_like(part_ref)

        for index in range(slots):
            pltpu.make_async_copy(zeros, give(index), out_sems.at[index]).wait()
        half_copy.wait()

    any_spec, vmem = pl.BlockSpec(memory_space=pl.ANY), pl.BlockSpec(memory_space=pltpu.VMEM)
    return pl.pallas_call(
        body,
        out_shape=(
            jax.ShapeDtypeStruct((2, half, share, width), BF16),
            jax.ShapeDtypeStruct((rows, share, width), BF16),
            jax.ShapeDtypeStruct((slots * width + half * share, width), BF16),
        ),
        in_specs=[pl.BlockSpec(memory_space=pltpu.SMEM), any_spec, any_spec, any_spec],
        out_specs=(vmem, vmem, any_spec),
        scratch_shapes=[
            pltpu.VMEM((steps, width, loads // steps), BF16),
            pltpu.VMEM((width, width), BF16),
            pltpu.VMEM(blocks.shape, BF16),
            pltpu.VMEM((width, width), BF16),
            pltpu.VMEM((half * share, width), BF16),
            pltpu.SemaphoreType.DMA((steps + 1,)),
            pltpu.SemaphoreType.DMA((levels,)),
            pltpu.SemaphoreType.DMA((slots + 1,)),
        ],
        compiler_params=pltpu.CompilerParams(vmem_limit_bytes=FIRST),
        cost_estimate=pl.CostEstimate(
            flops=4 * width * width * loads, bytes_accessed=2_200_000, transcendentals=0
        ),
    )(targets, rhs_low, inv_low, blocks)


def prepared(place, rhs_low, inv_low, answer0, level):
    _, held, share, width = answer0.shape
    lanes = max(share, 128)
    per_lanes = lanes // share

    def body(
        place_ref, rhs_ref, inv_ref, answer0_ref, kept_ref, out_ref, inverse_ref, first_ref, half_ref
    ):
        turned = rhs_ref[0].astype(F32).T
        picked = turned[:share]
        for other in range(1, per_lanes):
            picked = jnp.where(
                place_ref[0] % per_lanes == other,
                turned[other * share : (other + 1) * share],
                picked,
            )
        out_ref[...] = picked.astype(BF16)
        inverse_ref[...] = inv_ref[0]
        first_ref[...] = answer0_ref[0, 0]
        half_ref[...] = kept_ref[0].reshape(held * share, width)

    return pl.pallas_call(
        body,
        out_shape=(
            jax.ShapeDtypeStruct((share, width), BF16),
            jax.ShapeDtypeStruct((width, width), BF16),
            jax.ShapeDtypeStruct((share, width), BF16),
            jax.ShapeDtypeStruct((held * share, width), BF16),
        ),
        grid_spec=pltpu.PrefetchScalarGridSpec(
            num_scalar_prefetch=1,
            grid=(1,),
            in_specs=[
                pl.BlockSpec((1, width, lanes), lambda i, p: (level, 0, p[0] // per_lanes)),
                pl.BlockSpec((1, width, width), lambda i, p: (level, 0, 0)),
                pl.BlockSpec((1, 1, share, width), lambda i, p: (p[0] % 2, p[0] // 2, 0, 0)),
                pl.BlockSpec((1, held, share, width), lambda i, p: (p[1], 0, 0, 0)),
            ],
            out_specs=(
                pl.BlockSpec((share, width), lambda i, p: (0, 0)),
                pl.BlockSpec((width, width), lambda i, p: (0, 0)),
                pl.BlockSpec((share, width), lambda i, p: (0, 0)),
                pl.BlockSpec((held * share, width), lambda i, p: (0, 0)),
            ),
        ),
        compiler_params=pltpu.CompilerParams(vmem_limit_bytes=SMALL),
        cost_estimate=pl.CostEstimate(
            flops=width * width * 1000, bytes_accessed=2_000_000, transcendentals=0
        ),
    )(place, rhs_low, inv_low, answer0, answer0)


def summed_up(shares):
    def body(shares_ref, out_ref):
        out_ref[...] = jnp.sum(shares_ref[...].astype(F32), axis=0).astype(BF16)

    return pl.pallas_call(
        body,
        out_shape=jax.ShapeDtypeStruct(shares.shape[1:], BF16),
        compiler_params=pltpu.CompilerParams(vmem_limit_bytes=SMALL),
        cost_estimate=pl.CostEstimate(flops=200_000, bytes_accessed=450_000, transcendentals=0),
    )(shares)


def second_level(part, right_side, inverse, first, copies):
    share, width = part.shape

    def body(part_ref, rhs_ref, inv_ref, first_ref, answer_ref, both_ref):
        residual = (rhs_ref[...].astype(F32) - part_ref[...].astype(F32)).astype(BF16)
        answer = dot_nt(residual, inv_ref[...]).astype(BF16)
        for copy in range(copies):
            answer_ref[copy] = answer
        both_ref[0] = first_ref[...]
        both_ref[1] = answer

    return pl.pallas_call(
        body,
        out_shape=(
            jax.ShapeDtypeStruct((copies, share, width), BF16),
            jax.ShapeDtypeStruct((2, share, width), BF16),
        ),
        compiler_params=pltpu.CompilerParams(vmem_limit_bytes=SMALL),
        cost_estimate=pl.CostEstimate(
            flops=2 * width * width * share, bytes_accessed=600_000, transcendentals=0
        ),
    )(part, right_side, inverse, first)


def ancestor_parts(place, terms, count, loads, before=None):
    width = terms[0][1].shape[-1]

    def body(place_ref, *refs):
        answers, blocks, rest = refs[: len(terms)], refs[len(terms) : 2 * len(terms)], refs[2 * len(terms) :]
        total = None
        for answer, block in zip(answers, blocks):
            product = dot_nt(answer[...].reshape(loads, width), block[...])
            total = product if total is None else total + product
        if before is not None:
            total += rest[0][...].astype(F32)
        rest[-1][...] = total.astype(BF16)

    def answer_spec(answer, spot):
        if spot is None:
            return pl.BlockSpec((1, *answer.shape[1:]), lambda a, p: (p[1], 0, 0, 0))
        return pl.BlockSpec((loads, width), lambda a, p: (spot, 0))

    def block_spec(level):
        return pl.BlockSpec((width, width), lambda a, p: (level * count + a, 0))

    out_spec = pl.BlockSpec((loads, width), lambda a, p: (0, a))
    in_specs = [answer_spec(term[2], term[3]) for term in terms]
    in_specs += [block_spec(term[0]) for term in terms]
    operands = [term[2] for term in terms] + [term[1] for term in terms]
    if before is not None:
        in_specs.append(out_spec)
        operands.append(before)
    return pl.pallas_call(
        body,
        out_shape=jax.ShapeDtypeStruct((loads, count * width), BF16),
        grid_spec=pltpu.PrefetchScalarGridSpec(
            num_scalar_prefetch=1, grid=(count,), in_specs=in_specs, out_specs=out_spec
        ),
        compiler_params=pltpu.CompilerParams(vmem_limit_bytes=LARGE),
        cost_estimate=pl.CostEstimate(
            flops=2 * len(terms) * count * width * width * loads,
            bytes_accessed=5_000_000,
            transcendentals=0,
        ),
    )(place, *operands)


def ancestor_solve(arrived, rhs_anc, inv_anc):
    sources, loads, _ = arrived.shape
    count, _, width = rhs_anc.shape

    def body(arrived_ref, rhs_ref, inv_ref, out_ref):
        total = jnp.sum(arrived_ref[...].astype(F32), axis=0)
        residual = (rhs_ref[0].astype(F32) - total).astype(BF16)
        out_ref[0] = dot_nt(residual, inv_ref[0])

    return pl.pallas_call(
        body,
        out_shape=jax.ShapeDtypeStruct((count, loads, width), F32),
        grid=(count,),
        in_specs=[
            pl.BlockSpec((sources, loads, width), lambda a: (0, 0, a)),
            pl.BlockSpec((1, loads, width), lambda a: (a, 0, 0)),
            pl.BlockSpec((1, width, width), lambda a: (a, 0, 0)),
        ],
        out_specs=pl.BlockSpec((1, loads, width), lambda a: (a, 0, 0)),
        compiler_params=pltpu.CompilerParams(vmem_limit_bytes=LARGE),
        cost_estimate=pl.CostEstimate(
            flops=2 * count * width * width * loads, bytes_accessed=3_000_000, transcendentals=0
        ),
    )(arrived, rhs_anc, inv_anc)


def on_device(rhs_low, inv_low, blocks, targets, rhs_anc, inv_anc):
    rows, cols = lax.axis_size("row"), lax.axis_size("col")
    rhs_low, inv_low = rhs_low[0, :, 0], inv_low[0, :, 0]
    blocks, targets = blocks[0, 0, 0], targets[0, 0, 0]
    width, loads = rhs_low.shape[1:]
    layers = lax.axis_size("layer")
    place = jnp.stack([lax.axis_index("row"), lax.axis_index("layer") & 1]).astype(jnp.int32)

    answer0, part, give = first_level(targets, rhs_low, inv_low, blocks, rows)
    *ready, kept0 = prepared(place, rhs_low, inv_low, answer0, 1)
    shares = lax.all_to_all(part, "col", 0, 0, tiled=True)

    def neighbour(layer, row):
        ahead = (layer + row) % 2 == 0
        return (layer + (1 if ahead else -1)) % layers

    pairs = [
        (layer * rows + row, neighbour(layer, row) * rows + row)
        for layer in range(layers)
        for row in range(rows)
    ]

    def swap(value):
        return lax.ppermute(value, ("layer", "row"), pairs)

    near = swap(give)

    summed = summed_up(shares)
    turn = [
        (row * cols + col, col * cols + (row - 1) % rows)
        for row in range(rows)
        for col in range(cols)
    ]
    summed = lax.ppermute(summed, ("row", "col"), turn)
    pieces, both = second_level(summed, *ready, rows // 2)
    lines = [list(range(core, rows, 2)) for core in range(2)]
    chips = [[row, row + 1] for row in range(0, rows, 2)]
    pieces = lax.all_to_all(pieces, "row", 0, 0, axis_index_groups=lines, tiled=True)
    answer1 = lax.all_gather(pieces, "row", axis=0, axis_index_groups=chips)

    near_answer1 = swap(lax.dynamic_index_in_dim(answer1, 1 - place[1], 0, keepdims=False))
    wanted, count = loads // 2, inv_anc.shape[0]
    near_answer1 = near_answer1.reshape(wanted, width)
    own = [(0, give, kept0, 0), (1, give, answer1, None)]
    parts = ancestor_parts(place, own, count, wanted)
    far = [(0, near, near, near.shape[0] // wanted - 1), (1, near, near_answer1, 0)]
    parts = ancestor_parts(place, far, count, wanted, parts)
    groups = [
        [layer * cols + col for layer in range(parity, layers, 2) for col in range(cols)]
        for parity in range(2)
    ]
    members = len(groups[0])
    arrived = lax.all_to_all(
        parts.reshape(members, parts.shape[0] // members, -1),
        ("layer", "col"),
        0,
        0,
        axis_index_groups=groups,
        tiled=True,
    )
    solved = ancestor_solve(arrived, jnp.swapaxes(rhs_anc, 1, 2), inv_anc)
    return (jnp.swapaxes(both, 1, 2)[None, :, None], jnp.swapaxes(solved, 1, 2))


def solution(mesh):
    in_specs = (
        P("layer", None, "col", None, None),
        P("layer", None, "col", None, None),
        P("layer", "row", "col", None, None, None, None),
        P("layer", "row", "col", None, None),
        P("row", None, ("layer", "col")),
        P("row", None, None),
    )
    out_specs = (P("layer", None, "col", None, "row"), P("row", None, ("layer", "col")))
    return jax.shard_map(
        on_device, mesh=mesh, in_specs=in_specs, out_specs=out_specs, check_vma=False
    )
```

```python
import jax
import jax.numpy as jnp
from jax import lax
from jax.experimental import pallas as pl
from jax.experimental.pallas import tpu as pltpu
from jax.sharding import PartitionSpec as P

F32 = jnp.float32
BF16 = jnp.bfloat16
SMALL = 8 << 20
LARGE = 24 << 20
FIRST = 60 << 20
NT = (((1,), (1,)), ((), ()))


def dot_nt(left, right):
    return lax.dot_general(left, right, NT, preferred_element_type=F32)


def slot_of(targets_ref, level, target, per_row):
    slot, found = jnp.int32(0), jnp.int32(0)
    for member in range(per_row):
        hit = targets_ref[level, member] == target
        slot = jnp.where(hit, jnp.int32(member), slot)
        found = jnp.where(hit, jnp.int32(1), found)
    return slot, found


def first_level(targets, rhs_low, inv_low, blocks, rows):
    levels, width, loads = rhs_low.shape
    per_row = blocks.shape[1]
    share = loads // rows
    steps = 2
    held, half = rows // steps, rows // 2
    slots = levels * per_row
    lanes = max(share, 128)
    per_lanes = lanes // share

    def body(
        targets_ref, rhs_ref, inv_ref, blocks_ref, part_ref, kept_ref, ready_ref, give_ref,
        rhs_in, inv_in, next_in, blocks_in, zeros, half_out, in_sems, blocks_sems, out_sems,
    ):
        kept, row = lax.axis_index("layer") % 2, lax.axis_index("row")
        next_copy = pltpu.make_async_copy(
            rhs_ref.at[1, :, pl.ds(pl.multiple_of(row // per_lanes * lanes, lanes), lanes)],
            next_in,
            in_sems.at[steps + 1],
        )
        next_inverse = pltpu.make_async_copy(
            inv_ref.at[1], ready_ref.at[pl.ds(2 * share, width)], in_sems.at[steps + 2]
        )
        inv_copy = pltpu.make_async_copy(inv_ref.at[0], inv_in, in_sems.at[steps])
        rhs_copies = [
            pltpu.make_async_copy(
                rhs_ref.at[0, :, pl.ds(step * (loads // steps), loads // steps)],
                rhs_in.at[step],
                in_sems.at[step],
            )
            for step in range(steps)
        ]
        blocks_copies = [
            pltpu.make_async_copy(blocks_ref.at[level], blocks_in.at[level], blocks_sems.at[level])
            for level in range(levels)
        ]

        def give(index):
            return give_ref.at[pl.ds(index * width, width)]

        def pass_on(level):
            blocks_copies[level].wait()
            for ancestor in range(per_row):
                index = level * per_row + ancestor
                source, named = slot_of(targets_ref, level, ancestor + 2, per_row)

                @pl.when(named == 1)
                def _(index=index, source=source):
                    pltpu.make_async_copy(
                        blocks_in.at[level, source], give(index), out_sems.at[index]
                    ).start()

                @pl.when(named == 0)
                def _(index=index):
                    pltpu.make_async_copy(zeros, give(index), out_sems.at[index]).start()

        for copy in (inv_copy, *rhs_copies, *blocks_copies, next_copy, next_inverse):
            copy.start()
        zeros[...] = jnp.zeros_like(zeros)
        inv_copy.wait()
        answers = []
        for step in range(steps):
            if step > 0:
                pass_on(step - 1)
            rhs_copies[step].wait()
            answer = jnp.dot(inv_in[...], rhs_in[step], preferred_element_type=F32).T.astype(BF16)
            answers.append(answer)
            pieces = [answer[member * share : (member + 1) * share] for member in range(held)]
            for member in range(held):
                start = (step * (held // 2) + member // 2) * share

                @pl.when(kept == member % 2)
                def _(start=start, piece=pieces[member]):
                    kept_ref[start : start + share] = piece

                @pl.when(kept != member % 2)
                def _(start=start, piece=pieces[member]):
                    half_out[start : start + share] = piece

                @pl.when(row == step * held + member)
                def _(piece=pieces[member]):
                    ready_ref[share : 2 * share] = piece

        half_copy = pltpu.make_async_copy(
            half_out, give_ref.at[pl.ds(slots * width, half * share)], out_sems.at[slots]
        )
        half_copy.start()
        for level in range(steps - 1, levels):
            pass_on(level)
        slot, found = slot_of(targets_ref, 0, 1, per_row)

        @pl.when(found == 1)
        def _():
            for step in range(steps):
                part = dot_nt(answers[step], blocks_in[0, slot]).astype(BF16)
                part_ref[step * held : (step + 1) * held] = part.reshape(held, share, width)

        @pl.when(found == 0)
        def _():
            part_ref[...] = jnp.zeros_like(part_ref)

        next_copy.wait()
        turned = next_in[...].astype(F32).T
        picked = turned[:share]
        for other in range(1, per_lanes):
            picked = jnp.where(
                row % per_lanes == other, turned[other * share : (other + 1) * share], picked
            )
        ready_ref[:share] = picked.astype(BF16)
        next_inverse.wait()
        for index in range(slots):
            pltpu.make_async_copy(zeros, give(index), out_sems.at[index]).wait()
        half_copy.wait()

    any_spec, vmem = pl.BlockSpec(memory_space=pl.ANY), pl.BlockSpec(memory_space=pltpu.VMEM)
    return pl.pallas_call(
        body,
        out_shape=(
            jax.ShapeDtypeStruct((rows, share, width), BF16),
            jax.ShapeDtypeStruct((half * share, width), BF16),
            jax.ShapeDtypeStruct((2 * share + width, width), BF16),
            jax.ShapeDtypeStruct((slots * width + half * share, width), BF16),
        ),
        in_specs=[pl.BlockSpec(memory_space=pltpu.SMEM), any_spec, any_spec, any_spec],
        out_specs=(vmem, vmem, vmem, any_spec),
        scratch_shapes=[
            pltpu.VMEM((steps, width, loads // steps), BF16),
            pltpu.VMEM((width, width), BF16),
            pltpu.VMEM((width, lanes), BF16),
            pltpu.VMEM(blocks.shape, BF16),
            pltpu.VMEM((width, width), BF16),
            pltpu.VMEM((half * share, width), BF16),
            pltpu.SemaphoreType.DMA((steps + 3,)),
            pltpu.SemaphoreType.DMA((levels,)),
            pltpu.SemaphoreType.DMA((slots + 1,)),
        ],
        compiler_params=pltpu.CompilerParams(vmem_limit_bytes=FIRST),
        cost_estimate=pl.CostEstimate(
            flops=4 * width * width * loads, bytes_accessed=2_200_000, transcendentals=0
        ),
    )(targets, rhs_low, inv_low, blocks)


def summed_up(shares):
    def body(shares_ref, out_ref):
        out_ref[...] = jnp.sum(shares_ref[...].astype(F32), axis=0).astype(BF16)

    return pl.pallas_call(
        body,
        out_shape=jax.ShapeDtypeStruct(shares.shape[1:], BF16),
        compiler_params=pltpu.CompilerParams(vmem_limit_bytes=SMALL),
        cost_estimate=pl.CostEstimate(flops=200_000, bytes_accessed=450_000, transcendentals=0),
    )(shares)


def second_level(part, ready, copies):
    share, width = part.shape

    def body(part_ref, ready_ref, answer_ref, both_ref):
        residual = (ready_ref[:share].astype(F32) - part_ref[...].astype(F32)).astype(BF16)
        answer = dot_nt(residual, ready_ref[2 * share :]).astype(BF16)
        for copy in range(copies):
            answer_ref[copy] = answer
        both_ref[0] = ready_ref[share : 2 * share]
        both_ref[1] = answer

    return pl.pallas_call(
        body,
        out_shape=(
            jax.ShapeDtypeStruct((copies, share, width), BF16),
            jax.ShapeDtypeStruct((2, share, width), BF16),
        ),
        compiler_params=pltpu.CompilerParams(vmem_limit_bytes=SMALL),
        cost_estimate=pl.CostEstimate(
            flops=2 * width * width * share, bytes_accessed=600_000, transcendentals=0
        ),
    )(part, ready)


def ancestor_parts(place, terms, count, loads, before=None):
    width = terms[0][1].shape[-1]

    def body(place_ref, *refs):
        answers, blocks, rest = refs[: len(terms)], refs[len(terms) : 2 * len(terms)], refs[2 * len(terms) :]
        total = None
        for answer, block in zip(answers, blocks):
            product = dot_nt(answer[...].reshape(loads, width), block[...])
            total = product if total is None else total + product
        if before is not None:
            total += rest[0][...].astype(F32)
        rest[-1][...] = total.astype(BF16)

    def answer_spec(answer, spot):
        if spot is None:
            return pl.BlockSpec((1, *answer.shape[1:]), lambda a, p: (p[1], 0, 0, 0))
        return pl.BlockSpec((loads, width), lambda a, p: (spot, 0))

    def block_spec(level):
        return pl.BlockSpec((width, width), lambda a, p: (level * count + a, 0))

    out_spec = pl.BlockSpec((loads, width), lambda a, p: (0, a))
    in_specs = [answer_spec(term[2], term[3]) for term in terms]
    in_specs += [block_spec(term[0]) for term in terms]
    operands = [term[2] for term in terms] + [term[1] for term in terms]
    if before is not None:
        in_specs.append(out_spec)
        operands.append(before)
    return pl.pallas_call(
        body,
        out_shape=jax.ShapeDtypeStruct((loads, count * width), BF16),
        grid_spec=pltpu.PrefetchScalarGridSpec(
            num_scalar_prefetch=1, grid=(count,), in_specs=in_specs, out_specs=out_spec
        ),
        compiler_params=pltpu.CompilerParams(vmem_limit_bytes=LARGE),
        cost_estimate=pl.CostEstimate(
            flops=2 * len(terms) * count * width * width * loads,
            bytes_accessed=5_000_000,
            transcendentals=0,
        ),
    )(place, *operands)


def ancestor_solve(arrived, rhs_anc, inv_anc):
    sources, loads, _ = arrived.shape
    count, _, width = rhs_anc.shape

    def body(arrived_ref, rhs_ref, inv_ref, out_ref):
        total = jnp.sum(arrived_ref[...].astype(F32), axis=0)
        residual = (rhs_ref[0].astype(F32) - total).astype(BF16)
        out_ref[0] = dot_nt(residual, inv_ref[0])

    return pl.pallas_call(
        body,
        out_shape=jax.ShapeDtypeStruct((count, loads, width), F32),
        grid=(count,),
        in_specs=[
            pl.BlockSpec((sources, loads, width), lambda a: (0, 0, a)),
            pl.BlockSpec((1, loads, width), lambda a: (a, 0, 0)),
            pl.BlockSpec((1, width, width), lambda a: (a, 0, 0)),
        ],
        out_specs=pl.BlockSpec((1, loads, width), lambda a: (a, 0, 0)),
        compiler_params=pltpu.CompilerParams(vmem_limit_bytes=LARGE),
        cost_estimate=pl.CostEstimate(
            flops=2 * count * width * width * loads, bytes_accessed=3_000_000, transcendentals=0
        ),
    )(arrived, rhs_anc, inv_anc)


def on_device(rhs_low, inv_low, blocks, targets, rhs_anc, inv_anc):
    rows, cols = lax.axis_size("row"), lax.axis_size("col")
    rhs_low, inv_low = rhs_low[0, :, 0], inv_low[0, :, 0]
    blocks, targets = blocks[0, 0, 0], targets[0, 0, 0]
    width, loads = rhs_low.shape[1:]
    layers = lax.axis_size("layer")
    place = jnp.stack([lax.axis_index("row"), lax.axis_index("layer") & 1]).astype(jnp.int32)

    part, kept0, ready, give = first_level(targets, rhs_low, inv_low, blocks, rows)
    shares = lax.all_to_all(part, "col", 0, 0, tiled=True)

    def neighbour(layer, row):
        ahead = (layer + row) % 2 == 0
        return (layer + (1 if ahead else -1)) % layers

    pairs = [
        (layer * rows + row, neighbour(layer, row) * rows + row)
        for layer in range(layers)
        for row in range(rows)
    ]

    def swap(value):
        return lax.ppermute(value, ("layer", "row"), pairs)

    near = swap(give)

    summed = summed_up(shares)
    turn = [
        (row * cols + col, col * cols + (row - 1) % rows)
        for row in range(rows)
        for col in range(cols)
    ]
    summed = lax.ppermute(summed, ("row", "col"), turn)
    pieces, both = second_level(summed, ready, rows // 2)
    lines = [list(range(core, rows, 2)) for core in range(2)]
    chips = [[row, row + 1] for row in range(0, rows, 2)]
    pieces = lax.all_to_all(pieces, "row", 0, 0, axis_index_groups=lines, tiled=True)
    answer1 = lax.all_gather(pieces, "row", axis=0, axis_index_groups=chips)

    near_answer1 = swap(lax.dynamic_index_in_dim(answer1, 1 - place[1], 0, keepdims=False))
    wanted, count = loads // 2, inv_anc.shape[0]
    near_answer1 = near_answer1.reshape(wanted, width)
    own = [(0, give, kept0, 0), (1, give, answer1, None)]
    parts = ancestor_parts(place, own, count, wanted)
    far = [(0, near, near, near.shape[0] // wanted - 1), (1, near, near_answer1, 0)]
    parts = ancestor_parts(place, far, count, wanted, parts)
    groups = [
        [layer * cols + col for layer in range(parity, layers, 2) for col in range(cols)]
        for parity in range(2)
    ]
    members = len(groups[0])
    arrived = lax.all_to_all(
        parts.reshape(members, parts.shape[0] // members, -1),
        ("layer", "col"),
        0,
        0,
        axis_index_groups=groups,
        tiled=True,
    )
    solved = ancestor_solve(arrived, jnp.swapaxes(rhs_anc, 1, 2), inv_anc)
    return (jnp.swapaxes(both, 1, 2)[None, :, None], jnp.swapaxes(solved, 1, 2))


def solution(mesh):
    in_specs = (
        P("layer", None, "col", None, None),
        P("layer", None, "col", None, None),
        P("layer", "row", "col", None, None, None, None),
        P("layer", "row", "col", None, None),
        P("row", None, ("layer", "col")),
        P("row", None, None),
    )
    out_specs = (P("layer", None, "col", None, "row"), P("row", None, ("layer", "col")))
    return jax.shard_map(
        on_device, mesh=mesh, in_specs=in_specs, out_specs=out_specs, check_vma=False
    )
```

```python
import jax
import jax.numpy as jnp
from jax import lax
from jax.experimental import pallas as pl
from jax.experimental.pallas import tpu as pltpu
from jax.sharding import PartitionSpec as P

F32 = jnp.float32
BF16 = jnp.bfloat16
SMALL = 8 << 20
LARGE = 24 << 20
FIRST = 60 << 20
NT = (((1,), (1,)), ((), ()))


def dot_nt(left, right):
    return lax.dot_general(left, right, NT, preferred_element_type=F32)


def slot_of(targets_ref, level, target, per_row):
    slot, found = jnp.int32(0), jnp.int32(0)
    for member in range(per_row):
        hit = targets_ref[level, member] == target
        slot = jnp.where(hit, jnp.int32(member), slot)
        found = jnp.where(hit, jnp.int32(1), found)
    return slot, found


def first_level(targets, rhs_low, inv_low, blocks, rows):
    levels, width, loads = rhs_low.shape
    per_row = blocks.shape[1]
    share = loads // rows
    steps = 2
    held, half = rows // steps, rows // 2
    slots = levels * per_row
    lanes = max(share, 128)
    per_lanes = lanes // share

    def body(
        lists_ref, rhs_ref, inv_ref, blocks_ref, part_ref, kept_ref, ready_ref, give_ref,
        targets_ref, rhs_in, inv_in, next_in, blocks_in, zeros, half_out, in_sems, blocks_sems, out_sems,
    ):
        kept, row = lax.axis_index("layer") % 2, lax.axis_index("row")
        next_copy = pltpu.make_async_copy(
            rhs_ref.at[1, :, pl.ds(pl.multiple_of(row // per_lanes * lanes, lanes), lanes)],
            next_in,
            in_sems.at[steps + 1],
        )
        next_inverse = pltpu.make_async_copy(
            inv_ref.at[1], ready_ref.at[pl.ds(2 * share, width)], in_sems.at[steps + 2]
        )
        inv_copy = pltpu.make_async_copy(inv_ref.at[0], inv_in, in_sems.at[steps])
        rhs_copies = [
            pltpu.make_async_copy(
                rhs_ref.at[0, :, pl.ds(step * (loads // steps), loads // steps)],
                rhs_in.at[step],
                in_sems.at[step],
            )
            for step in range(steps)
        ]
        blocks_copies = [
            pltpu.make_async_copy(blocks_ref.at[level], blocks_in.at[level], blocks_sems.at[level])
            for level in range(levels)
        ]

        def give(index):
            return give_ref.at[pl.ds(index * width, width)]

        def pass_on(level):
            blocks_copies[level].wait()
            for ancestor in range(per_row):
                index = level * per_row + ancestor
                source, named = slot_of(targets_ref, level, ancestor + 2, per_row)

                @pl.when(named == 1)
                def _(index=index, source=source):
                    pltpu.make_async_copy(
                        blocks_in.at[level, source], give(index), out_sems.at[index]
                    ).start()

                @pl.when(named == 0)
                def _(index=index):
                    pltpu.make_async_copy(zeros, give(index), out_sems.at[index]).start()

        lists_copy = pltpu.make_async_copy(lists_ref, targets_ref, in_sems.at[steps + 3])
        for copy in (inv_copy, *rhs_copies, lists_copy, *blocks_copies, next_copy, next_inverse):
            copy.start()
        zeros[...] = jnp.zeros_like(zeros)
        lists_copy.wait()
        inv_copy.wait()
        answers = []
        for step in range(steps):
            if step > 0:
                pass_on(step - 1)
            rhs_copies[step].wait()
            answer = jnp.dot(inv_in[...], rhs_in[step], preferred_element_type=F32).T.astype(BF16)
            answers.append(answer)
            pieces = [answer[member * share : (member + 1) * share] for member in range(held)]
            for member in range(held):
                start = (step * (held // 2) + member // 2) * share

                @pl.when(kept == member % 2)
                def _(start=start, piece=pieces[member]):
                    kept_ref[start : start + share] = piece

                @pl.when(kept != member % 2)
                def _(start=start, piece=pieces[member]):
                    half_out[start : start + share] = piece

                @pl.when(row == step * held + member)
                def _(piece=pieces[member]):
                    ready_ref[share : 2 * share] = piece

        half_copy = pltpu.make_async_copy(
            half_out, give_ref.at[pl.ds(slots * width, half * share)], out_sems.at[slots]
        )
        half_copy.start()
        for level in range(steps - 1, levels):
            pass_on(level)
        slot, found = slot_of(targets_ref, 0, 1, per_row)

        @pl.when(found == 1)
        def _():
            for step in range(steps):
                part = dot_nt(answers[step], blocks_in[0, slot]).astype(BF16)
                part_ref[step * held : (step + 1) * held] = part.reshape(held, share, width)

        @pl.when(found == 0)
        def _():
            part_ref[...] = jnp.zeros_like(part_ref)

        next_copy.wait()
        turned = next_in[...].astype(F32).T
        picked = turned[:share]
        for other in range(1, per_lanes):
            picked = jnp.where(
                row % per_lanes == other, turned[other * share : (other + 1) * share], picked
            )
        ready_ref[:share] = picked.astype(BF16)
        next_inverse.wait()
        for index in range(slots):
            pltpu.make_async_copy(zeros, give(index), out_sems.at[index]).wait()
        half_copy.wait()

    any_spec, vmem = pl.BlockSpec(memory_space=pl.ANY), pl.BlockSpec(memory_space=pltpu.VMEM)
    return pl.pallas_call(
        body,
        out_shape=(
            jax.ShapeDtypeStruct((rows, share, width), BF16),
            jax.ShapeDtypeStruct((half * share, width), BF16),
            jax.ShapeDtypeStruct((2 * share + width, width), BF16),
            jax.ShapeDtypeStruct((slots * width + half * share, width), BF16),
        ),
        in_specs=[any_spec] * 4,
        out_specs=(vmem, vmem, vmem, any_spec),
        scratch_shapes=[
            pltpu.SMEM(targets.shape, targets.dtype),
            pltpu.VMEM((steps, width, loads // steps), BF16),
            pltpu.VMEM((width, width), BF16),
            pltpu.VMEM((width, lanes), BF16),
            pltpu.VMEM(blocks.shape, BF16),
            pltpu.VMEM((width, width), BF16),
            pltpu.VMEM((half * share, width), BF16),
            pltpu.SemaphoreType.DMA((steps + 4,)),
            pltpu.SemaphoreType.DMA((levels,)),
            pltpu.SemaphoreType.DMA((slots + 1,)),
        ],
        compiler_params=pltpu.CompilerParams(vmem_limit_bytes=FIRST),
        cost_estimate=pl.CostEstimate(
            flops=4 * width * width * loads, bytes_accessed=2_200_000, transcendentals=0
        ),
    )(targets, rhs_low, inv_low, blocks)


def summed_up(shares):
    def body(shares_ref, out_ref):
        out_ref[...] = jnp.sum(shares_ref[...].astype(F32), axis=0).astype(BF16)

    return pl.pallas_call(
        body,
        out_shape=jax.ShapeDtypeStruct(shares.shape[1:], BF16),
        compiler_params=pltpu.CompilerParams(vmem_limit_bytes=SMALL),
        cost_estimate=pl.CostEstimate(flops=200_000, bytes_accessed=450_000, transcendentals=0),
    )(shares)


def second_level(part, ready, copies):
    share, width = part.shape

    def body(part_ref, ready_ref, answer_ref, both_ref):
        residual = (ready_ref[:share].astype(F32) - part_ref[...].astype(F32)).astype(BF16)
        answer = dot_nt(residual, ready_ref[2 * share :]).astype(BF16)
        for copy in range(copies):
            answer_ref[copy] = answer
        both_ref[0] = ready_ref[share : 2 * share]
        both_ref[1] = answer

    return pl.pallas_call(
        body,
        out_shape=(
            jax.ShapeDtypeStruct((copies, share, width), BF16),
            jax.ShapeDtypeStruct((2, share, width), BF16),
        ),
        compiler_params=pltpu.CompilerParams(vmem_limit_bytes=SMALL),
        cost_estimate=pl.CostEstimate(
            flops=2 * width * width * share, bytes_accessed=600_000, transcendentals=0
        ),
    )(part, ready)


def ancestor_parts(terms, count, loads, before=None):
    width = terms[0][1].shape[-1]

    def body(*refs):
        answers, blocks, rest = refs[: len(terms)], refs[len(terms) : 2 * len(terms)], refs[2 * len(terms) :]
        total = None
        for answer, block in zip(answers, blocks):
            product = dot_nt(answer[...], block[...])
            total = product if total is None else total + product
        if before is not None:
            total += rest[0][...].astype(F32)
        rest[-1][...] = total.astype(BF16)

    def answer_spec(spot):
        return pl.BlockSpec((loads, width), lambda a: (spot, 0))

    def block_spec(level):
        return pl.BlockSpec((width, width), lambda a: (level * count + a, 0))

    out_spec = pl.BlockSpec((loads, width), lambda a: (0, a))
    in_specs = [answer_spec(term[3]) for term in terms]
    in_specs += [block_spec(term[0]) for term in terms]
    operands = [term[2] for term in terms] + [term[1] for term in terms]
    if before is not None:
        in_specs.append(out_spec)
        operands.append(before)
    return pl.pallas_call(
        body,
        out_shape=jax.ShapeDtypeStruct((loads, count * width), BF16),
        grid=(count,),
        in_specs=in_specs,
        out_specs=out_spec,
        compiler_params=pltpu.CompilerParams(vmem_limit_bytes=LARGE),
        cost_estimate=pl.CostEstimate(
            flops=2 * len(terms) * count * width * width * loads,
            bytes_accessed=5_000_000,
            transcendentals=0,
        ),
    )(*operands)


def ancestor_solve(arrived, rhs_anc, inv_anc):
    sources, loads, _ = arrived.shape
    count, _, width = rhs_anc.shape

    def body(arrived_ref, rhs_ref, inv_ref, out_ref):
        total = jnp.sum(arrived_ref[...].astype(F32), axis=0)
        residual = (rhs_ref[0].astype(F32) - total).astype(BF16)
        out_ref[0] = dot_nt(residual, inv_ref[0])

    return pl.pallas_call(
        body,
        out_shape=jax.ShapeDtypeStruct((count, loads, width), F32),
        grid=(count,),
        in_specs=[
            pl.BlockSpec((sources, loads, width), lambda a: (0, 0, a)),
            pl.BlockSpec((1, loads, width), lambda a: (a, 0, 0)),
            pl.BlockSpec((1, width, width), lambda a: (a, 0, 0)),
        ],
        out_specs=pl.BlockSpec((1, loads, width), lambda a: (a, 0, 0)),
        compiler_params=pltpu.CompilerParams(vmem_limit_bytes=LARGE),
        cost_estimate=pl.CostEstimate(
            flops=2 * count * width * width * loads, bytes_accessed=3_000_000, transcendentals=0
        ),
    )(arrived, rhs_anc, inv_anc)


def on_device(rhs_low, inv_low, blocks, targets, rhs_anc, inv_anc):
    rows, cols = lax.axis_size("row"), lax.axis_size("col")
    rhs_low, inv_low = rhs_low[0, :, 0], inv_low[0, :, 0]
    blocks, targets = blocks[0, 0, 0], targets[0, 0, 0]
    width, loads = rhs_low.shape[1:]
    layers = lax.axis_size("layer")
    kept = lax.axis_index("layer") & 1

    part, kept0, ready, give = first_level(targets, rhs_low, inv_low, blocks, rows)
    shares = lax.all_to_all(part, "col", 0, 0, tiled=True)

    def neighbour(layer, row):
        ahead = (layer + row) % 2 == 0
        return (layer + (1 if ahead else -1)) % layers

    pairs = [
        (layer * rows + row, neighbour(layer, row) * rows + row)
        for layer in range(layers)
        for row in range(rows)
    ]

    def swap(value):
        return lax.ppermute(value, ("layer", "row"), pairs)

    near = swap(give)

    summed = summed_up(shares)
    turn = [
        (row * cols + col, col * cols + (row - 1) % rows)
        for row in range(rows)
        for col in range(cols)
    ]
    summed = lax.ppermute(summed, ("row", "col"), turn)
    pieces, both = second_level(summed, ready, rows // 2)
    lines = [list(range(core, rows, 2)) for core in range(2)]
    chips = [[row, row + 1] for row in range(0, rows, 2)]
    pieces = lax.all_to_all(pieces, "row", 0, 0, axis_index_groups=lines, tiled=True)
    answer1 = lax.all_gather(pieces, "row", axis=0, axis_index_groups=chips)

    wanted, count = loads // 2, inv_anc.shape[0]

    def half_of(parity):
        half = lax.dynamic_index_in_dim(answer1, parity, 0, keepdims=False)
        return half.reshape(wanted, width)

    near_answer1 = swap(half_of(1 - kept))
    early = [
        (0, give, kept0, 0),
        (1, give, half_of(kept), 0),
        (0, near, near, near.shape[0] // wanted - 1),
    ]
    parts = ancestor_parts(early, count, wanted)
    parts = ancestor_parts([(1, near, near_answer1, 0)], count, wanted, parts)
    groups = [
        [layer * cols + col for layer in range(parity, layers, 2) for col in range(cols)]
        for parity in range(2)
    ]
    members = len(groups[0])
    arrived = lax.all_to_all(
        parts.reshape(members, parts.shape[0] // members, -1),
        ("layer", "col"),
        0,
        0,
        axis_index_groups=groups,
        tiled=True,
    )
    solved = ancestor_solve(arrived, jnp.swapaxes(rhs_anc, 1, 2), inv_anc)
    return (jnp.swapaxes(both, 1, 2)[None, :, None], jnp.swapaxes(solved, 1, 2))


def solution(mesh):
    in_specs = (
        P("layer", None, "col", None, None),
        P("layer", None, "col", None, None),
        P("layer", "row", "col", None, None, None, None),
        P("layer", "row", "col", None, None),
        P("row", None, ("layer", "col")),
        P("row", None, None),
    )
    out_specs = (P("layer", None, "col", None, "row"), P("row", None, ("layer", "col")))
    return jax.shard_map(
        on_device, mesh=mesh, in_specs=in_specs, out_specs=out_specs, check_vma=False
    )
```

```python
import jax
import jax.numpy as jnp
from jax import lax
from jax.experimental import pallas as pl
from jax.experimental.pallas import tpu as pltpu
from jax.sharding import PartitionSpec as P

F32 = jnp.float32
BF16 = jnp.bfloat16
SMALL = 8 << 20
LARGE = 24 << 20
FIRST = 60 << 20
NT = (((1,), (1,)), ((), ()))


def dot_nt(left, right):
    return lax.dot_general(left, right, NT, preferred_element_type=F32)


def slot_of(targets_ref, level, target, per_row):
    slot, found = jnp.int32(0), jnp.int32(0)
    for member in range(per_row):
        hit = targets_ref[level, member] == target
        slot = jnp.where(hit, jnp.int32(member), slot)
        found = jnp.where(hit, jnp.int32(1), found)
    return slot, found


def first_level(targets, rhs_low, inv_low, blocks, rows):
    levels, width, loads = rhs_low.shape
    per_row = blocks.shape[1]
    share = loads // rows
    steps = 2
    held, half = rows // steps, rows // 2
    slots = levels * per_row
    lanes = max(share, 128)
    per_lanes = lanes // share

    def body(
        lists_ref, rhs_ref, inv_ref, blocks_ref, part_ref, kept_ref, ready_ref, give_ref,
        targets_ref, rhs_in, inv_in, next_in, blocks_in, zeros, half_out, in_sems, blocks_sems, out_sems,
    ):
        kept, row = lax.axis_index("layer") % 2, lax.axis_index("row")
        next_copy = pltpu.make_async_copy(
            rhs_ref.at[1, :, pl.ds(pl.multiple_of(row // per_lanes * lanes, lanes), lanes)],
            next_in,
            in_sems.at[steps + 1],
        )
        next_inverse = pltpu.make_async_copy(
            inv_ref.at[1], ready_ref.at[pl.ds(2 * share, width)], in_sems.at[steps + 2]
        )
        inv_copy = pltpu.make_async_copy(inv_ref.at[0], inv_in, in_sems.at[steps])
        rhs_copies = [
            pltpu.make_async_copy(
                rhs_ref.at[0, :, pl.ds(step * (loads // steps), loads // steps)],
                rhs_in.at[step],
                in_sems.at[step],
            )
            for step in range(steps)
        ]
        blocks_copies = [
            pltpu.make_async_copy(blocks_ref.at[level], blocks_in.at[level], blocks_sems.at[level])
            for level in range(levels)
        ]

        def give(index):
            return give_ref.at[pl.ds(index * width, width)]

        def pass_on(level):
            blocks_copies[level].wait()
            for ancestor in range(per_row):
                index = level * per_row + ancestor
                source, named = slot_of(targets_ref, level, ancestor + 2, per_row)

                @pl.when(named == 1)
                def _(index=index, source=source):
                    pltpu.make_async_copy(
                        blocks_in.at[level, source], give(index), out_sems.at[index]
                    ).start()

                @pl.when(named == 0)
                def _(index=index):
                    pltpu.make_async_copy(zeros, give(index), out_sems.at[index]).start()

        lists_copy = pltpu.make_async_copy(lists_ref, targets_ref, in_sems.at[steps + 3])
        for copy in (inv_copy, *rhs_copies, lists_copy, *blocks_copies, next_copy, next_inverse):
            copy.start()
        zeros[...] = jnp.zeros_like(zeros)
        lists_copy.wait()
        inv_copy.wait()
        answers = []
        for step in range(steps):
            if step > 0:
                pass_on(step - 1)
            rhs_copies[step].wait()
            answer = jnp.dot(inv_in[...], rhs_in[step], preferred_element_type=F32).T.astype(BF16)
            answers.append(answer)
            pieces = [answer[member * share : (member + 1) * share] for member in range(held)]
            for member in range(held):
                start = (step * (held // 2) + member // 2) * share

                @pl.when(kept == member % 2)
                def _(start=start, piece=pieces[member]):
                    kept_ref[start : start + share] = piece

                @pl.when(kept != member % 2)
                def _(start=start, piece=pieces[member]):
                    half_out[start : start + share] = piece

                @pl.when(row == step * held + member)
                def _(piece=pieces[member]):
                    ready_ref[share : 2 * share] = piece

        half_copy = pltpu.make_async_copy(
            half_out, give_ref.at[pl.ds(slots * width, half * share)], out_sems.at[slots]
        )
        half_copy.start()
        for level in range(steps - 1, levels):
            pass_on(level)
        slot, found = slot_of(targets_ref, 0, 1, per_row)

        @pl.when(found == 1)
        def _():
            for step in range(steps):
                part = dot_nt(answers[step], blocks_in[0, slot]).astype(BF16)
                part_ref[step * held : (step + 1) * held] = part.reshape(held, share, width)

        @pl.when(found == 0)
        def _():
            part_ref[...] = jnp.zeros_like(part_ref)

        next_copy.wait()
        turned = next_in[...].astype(F32).T
        picked = turned[:share]
        for other in range(1, per_lanes):
            picked = jnp.where(
                row % per_lanes == other, turned[other * share : (other + 1) * share], picked
            )
        ready_ref[:share] = picked.astype(BF16)
        next_inverse.wait()
        for index in range(slots):
            pltpu.make_async_copy(zeros, give(index), out_sems.at[index]).wait()
        half_copy.wait()

    any_spec, vmem = pl.BlockSpec(memory_space=pl.ANY), pl.BlockSpec(memory_space=pltpu.VMEM)
    return pl.pallas_call(
        body,
        out_shape=(
            jax.ShapeDtypeStruct((rows, share, width), BF16),
            jax.ShapeDtypeStruct((half * share, width), BF16),
            jax.ShapeDtypeStruct((2 * share + width, width), BF16),
            jax.ShapeDtypeStruct((slots * width + half * share, width), BF16),
        ),
        in_specs=[any_spec] * 4,
        out_specs=(vmem, vmem, vmem, any_spec),
        scratch_shapes=[
            pltpu.SMEM(targets.shape, targets.dtype),
            pltpu.VMEM((steps, width, loads // steps), BF16),
            pltpu.VMEM((width, width), BF16),
            pltpu.VMEM((width, lanes), BF16),
            pltpu.VMEM(blocks.shape, BF16),
            pltpu.VMEM((width, width), BF16),
            pltpu.VMEM((half * share, width), BF16),
            pltpu.SemaphoreType.DMA((steps + 4,)),
            pltpu.SemaphoreType.DMA((levels,)),
            pltpu.SemaphoreType.DMA((slots + 1,)),
        ],
        compiler_params=pltpu.CompilerParams(vmem_limit_bytes=FIRST),
        cost_estimate=pl.CostEstimate(
            flops=4 * width * width * loads, bytes_accessed=2_200_000, transcendentals=0
        ),
    )(targets, rhs_low, inv_low, blocks)


def summed_up(shares):
    def body(shares_ref, out_ref):
        out_ref[...] = jnp.sum(shares_ref[...].astype(F32), axis=0).astype(BF16)

    return pl.pallas_call(
        body,
        out_shape=jax.ShapeDtypeStruct(shares.shape[1:], BF16),
        compiler_params=pltpu.CompilerParams(vmem_limit_bytes=SMALL),
        cost_estimate=pl.CostEstimate(flops=200_000, bytes_accessed=450_000, transcendentals=0),
    )(shares)


def second_level(part, ready, copies):
    share, width = part.shape

    def body(part_ref, ready_ref, answer_ref, both_ref):
        residual = (ready_ref[:share].astype(F32) - part_ref[...].astype(F32)).astype(BF16)
        answer = dot_nt(residual, ready_ref[2 * share :]).astype(BF16)
        for copy in range(copies):
            answer_ref[copy] = answer
        both_ref[0] = ready_ref[share : 2 * share]
        both_ref[1] = answer

    return pl.pallas_call(
        body,
        out_shape=(
            jax.ShapeDtypeStruct((copies, share, width), BF16),
            jax.ShapeDtypeStruct((2, share, width), BF16),
        ),
        compiler_params=pltpu.CompilerParams(vmem_limit_bytes=SMALL),
        cost_estimate=pl.CostEstimate(
            flops=2 * width * width * share, bytes_accessed=600_000, transcendentals=0
        ),
    )(part, ready)


def ancestor_parts(terms, count, loads, before=None):
    width = terms[0][1].shape[-1]
    arrays = []
    for _, blocks, answer, _ in terms:
        arrays += [array for array in (blocks, answer) if all(array is not held for held in arrays)]
    places = [
        [next(i for i, held in enumerate(arrays) if held is array) for array in term[1:3]]
        for term in terms
    ]

    def body(*refs):
        out_ref = refs[-1]
        for ancestor in range(count):
            columns = slice(ancestor * width, (ancestor + 1) * width)
            total = None
            for (level, _, _, spot), (blocks, answer) in zip(terms, places):
                start = (level * count + ancestor) * width
                product = dot_nt(
                    refs[answer][spot * loads : (spot + 1) * loads],
                    refs[blocks][start : start + width],
                )
                total = product if total is None else total + product
            if before is not None:
                total += refs[len(arrays)][:, columns].astype(F32)
            out_ref[:, columns] = total.astype(BF16)

    operands = arrays if before is None else [*arrays, before]
    vmem = pl.BlockSpec(memory_space=pltpu.VMEM)
    return pl.pallas_call(
        body,
        out_shape=jax.ShapeDtypeStruct((loads, count * width), BF16),
        in_specs=[vmem] * len(operands),
        out_specs=vmem,
        compiler_params=pltpu.CompilerParams(vmem_limit_bytes=LARGE),
        cost_estimate=pl.CostEstimate(
            flops=2 * len(terms) * count * width * width * loads,
            bytes_accessed=5_000_000,
            transcendentals=0,
        ),
    )(*operands)


def ancestor_solve(arrived, rhs_anc, inv_anc):
    sources, loads, _ = arrived.shape
    count, _, width = rhs_anc.shape

    def body(arrived_ref, rhs_ref, inv_ref, out_ref):
        for ancestor in range(count):
            columns = slice(ancestor * width, (ancestor + 1) * width)
            total = jnp.sum(arrived_ref[:, :, columns].astype(F32), axis=0)
            residual = (rhs_ref[ancestor].astype(F32) - total).astype(BF16)
            out_ref[ancestor] = dot_nt(residual, inv_ref[ancestor])

    vmem = pl.BlockSpec(memory_space=pltpu.VMEM)
    return pl.pallas_call(
        body,
        out_shape=jax.ShapeDtypeStruct((count, loads, width), F32),
        in_specs=[vmem] * 3,
        out_specs=vmem,
        compiler_params=pltpu.CompilerParams(vmem_limit_bytes=LARGE),
        cost_estimate=pl.CostEstimate(
            flops=2 * count * width * width * loads, bytes_accessed=3_000_000, transcendentals=0
        ),
    )(arrived, rhs_anc, inv_anc)


def on_device(rhs_low, inv_low, blocks, targets, rhs_anc, inv_anc):
    rows, cols = lax.axis_size("row"), lax.axis_size("col")
    rhs_low, inv_low = rhs_low[0, :, 0], inv_low[0, :, 0]
    blocks, targets = blocks[0, 0, 0], targets[0, 0, 0]
    width, loads = rhs_low.shape[1:]
    layers = lax.axis_size("layer")
    kept = lax.axis_index("layer") & 1

    part, kept0, ready, give = first_level(targets, rhs_low, inv_low, blocks, rows)
    shares = lax.all_to_all(part, "col", 0, 0, tiled=True)

    def neighbour(layer, row):
        ahead = (layer + row) % 2 == 0
        return (layer + (1 if ahead else -1)) % layers

    pairs = [
        (layer * rows + row, neighbour(layer, row) * rows + row)
        for layer in range(layers)
        for row in range(rows)
    ]

    def swap(value):
        return lax.ppermute(value, ("layer", "row"), pairs)

    near = swap(give)

    summed = summed_up(shares)
    turn = [
        (row * cols + col, col * cols + (row - 1) % rows)
        for row in range(rows)
        for col in range(cols)
    ]
    summed = lax.ppermute(summed, ("row", "col"), turn)
    pieces, both = second_level(summed, ready, rows // 2)
    lines = [list(range(core, rows, 2)) for core in range(2)]
    chips = [[row, row + 1] for row in range(0, rows, 2)]
    pieces = lax.all_to_all(pieces, "row", 0, 0, axis_index_groups=lines, tiled=True)
    answer1 = lax.all_gather(pieces, "row", axis=0, axis_index_groups=chips)

    wanted, count = loads // 2, inv_anc.shape[0]

    def half_of(parity):
        half = lax.dynamic_index_in_dim(answer1, parity, 0, keepdims=False)
        return half.reshape(wanted, width)

    near_answer1 = swap(half_of(1 - kept))
    early = [
        (0, give, kept0, 0),
        (1, give, half_of(kept), 0),
        (0, near, near, near.shape[0] // wanted - 1),
    ]
    parts = ancestor_parts(early, count, wanted)
    parts = ancestor_parts([(1, near, near_answer1, 0)], count, wanted, parts)
    groups = [
        [layer * cols + col for layer in range(parity, layers, 2) for col in range(cols)]
        for parity in range(2)
    ]
    members = len(groups[0])
    arrived = lax.all_to_all(
        parts.reshape(members, parts.shape[0] // members, -1),
        ("layer", "col"),
        0,
        0,
        axis_index_groups=groups,
        tiled=True,
    )
    solved = ancestor_solve(arrived, jnp.swapaxes(rhs_anc, 1, 2), inv_anc)
    return (jnp.swapaxes(both, 1, 2)[None, :, None], jnp.swapaxes(solved, 1, 2))


def solution(mesh):
    in_specs = (
        P("layer", None, "col", None, None),
        P("layer", None, "col", None, None),
        P("layer", "row", "col", None, None, None, None),
        P("layer", "row", "col", None, None),
        P("row", None, ("layer", "col")),
        P("row", None, None),
    )
    out_specs = (P("layer", None, "col", None, "row"), P("row", None, ("layer", "col")))
    return jax.shard_map(
        on_device, mesh=mesh, in_specs=in_specs, out_specs=out_specs, check_vma=False
    )
```

```python
import jax
import jax.numpy as jnp
from jax import lax
from jax.experimental import pallas as pl
from jax.experimental.pallas import tpu as pltpu
from jax.sharding import PartitionSpec as P

F32 = jnp.float32
BF16 = jnp.bfloat16
SMALL = 8 << 20
LARGE = 24 << 20
FIRST = 60 << 20
NT = (((1,), (1,)), ((), ()))


def dot_nt(left, right):
    return lax.dot_general(left, right, NT, preferred_element_type=F32)


def slot_of(targets_ref, level, target, per_row):
    slot, found = jnp.int32(0), jnp.int32(0)
    for member in range(per_row):
        hit = targets_ref[level, member] == target
        slot = jnp.where(hit, jnp.int32(member), slot)
        found = jnp.where(hit, jnp.int32(1), found)
    return slot, found


def first_level(targets, rhs_low, inv_low, blocks, rows):
    levels, width, loads = rhs_low.shape
    per_row = blocks.shape[1]
    share = loads // rows
    steps = 2
    held, half = rows // steps, rows // 2
    slots = levels * per_row
    lanes = max(share, 128)
    per_lanes = lanes // share

    def body(
        lists_ref, rhs_ref, inv_ref, blocks_ref, part_ref, kept_ref, ready_ref, give_ref,
        targets_ref, rhs_in, inv_in, next_in, blocks_in, zeros, half_out, in_sems, blocks_sems, out_sems,
    ):
        kept, row = lax.axis_index("layer") % 2, lax.axis_index("row")
        next_copy = pltpu.make_async_copy(
            rhs_ref.at[1, :, pl.ds(pl.multiple_of(row // per_lanes * lanes, lanes), lanes)],
            next_in,
            in_sems.at[steps + 1],
        )
        next_inverse = pltpu.make_async_copy(
            inv_ref.at[1], ready_ref.at[pl.ds(2 * share, width)], in_sems.at[steps + 2]
        )
        inv_copy = pltpu.make_async_copy(inv_ref.at[0], inv_in, in_sems.at[steps])
        rhs_copies = [
            pltpu.make_async_copy(
                rhs_ref.at[0, :, pl.ds(step * (loads // steps), loads // steps)],
                rhs_in.at[step],
                in_sems.at[step],
            )
            for step in range(steps)
        ]
        blocks_copies = [
            pltpu.make_async_copy(blocks_ref.at[level], blocks_in.at[level], blocks_sems.at[level])
            for level in range(levels)
        ]

        def give(index):
            return give_ref.at[pl.ds(index * width, width)]

        def pass_on(level):
            blocks_copies[level].wait()
            for ancestor in range(per_row):
                index = level * per_row + ancestor
                source, named = slot_of(targets_ref, level, ancestor + 2, per_row)

                @pl.when(named == 1)
                def _(index=index, source=source):
                    pltpu.make_async_copy(
                        blocks_in.at[level, source], give(index), out_sems.at[index]
                    ).start()

                @pl.when(named == 0)
                def _(index=index):
                    pltpu.make_async_copy(zeros, give(index), out_sems.at[index]).start()

        lists_copy = pltpu.make_async_copy(lists_ref, targets_ref, in_sems.at[steps + 3])
        for copy in (inv_copy, *rhs_copies, lists_copy, *blocks_copies, next_copy, next_inverse):
            copy.start()
        zeros[...] = jnp.zeros_like(zeros)
        lists_copy.wait()
        inv_copy.wait()
        answers = []
        for step in range(steps):
            if step > 0:
                pass_on(step - 1)
            rhs_copies[step].wait()
            answer = jnp.dot(inv_in[...], rhs_in[step], preferred_element_type=F32).T.astype(BF16)
            answers.append(answer)
            pieces = [answer[member * share : (member + 1) * share] for member in range(held)]
            for member in range(held):
                start = (step * (held // 2) + member // 2) * share

                @pl.when(kept == member % 2)
                def _(start=start, piece=pieces[member]):
                    kept_ref[start : start + share] = piece

                @pl.when(kept != member % 2)
                def _(start=start, piece=pieces[member]):
                    half_out[start : start + share] = piece

                @pl.when(row == step * held + member)
                def _(piece=pieces[member]):
                    ready_ref[share : 2 * share] = piece

        half_copy = pltpu.make_async_copy(
            half_out, give_ref.at[pl.ds(slots * width, half * share)], out_sems.at[slots]
        )
        half_copy.start()
        for level in range(steps - 1, levels):
            pass_on(level)
        slot, found = slot_of(targets_ref, 0, 1, per_row)

        @pl.when(found == 1)
        def _():
            for step in range(steps):
                part = dot_nt(answers[step], blocks_in[0, slot]).astype(BF16)
                part_ref[step * held : (step + 1) * held] = part.reshape(held, share, width)

        @pl.when(found == 0)
        def _():
            part_ref[...] = jnp.zeros_like(part_ref)

        next_copy.wait()
        turned = next_in[...].astype(F32).T
        picked = turned[:share]
        for other in range(1, per_lanes):
            picked = jnp.where(
                row % per_lanes == other, turned[other * share : (other + 1) * share], picked
            )
        ready_ref[:share] = picked.astype(BF16)
        next_inverse.wait()
        for index in range(slots):
            pltpu.make_async_copy(zeros, give(index), out_sems.at[index]).wait()
        half_copy.wait()

    any_spec, vmem = pl.BlockSpec(memory_space=pl.ANY), pl.BlockSpec(memory_space=pltpu.VMEM)
    return pl.pallas_call(
        body,
        out_shape=(
            jax.ShapeDtypeStruct((rows, share, width), BF16),
            jax.ShapeDtypeStruct((half * share, width), BF16),
            jax.ShapeDtypeStruct((2 * share + width, width), BF16),
            jax.ShapeDtypeStruct((slots * width + half * share, width), BF16),
        ),
        in_specs=[any_spec] * 4,
        out_specs=(vmem, vmem, vmem, any_spec),
        scratch_shapes=[
            pltpu.SMEM(targets.shape, targets.dtype),
            pltpu.VMEM((steps, width, loads // steps), BF16),
            pltpu.VMEM((width, width), BF16),
            pltpu.VMEM((width, lanes), BF16),
            pltpu.VMEM(blocks.shape, BF16),
            pltpu.VMEM((width, width), BF16),
            pltpu.VMEM((half * share, width), BF16),
            pltpu.SemaphoreType.DMA((steps + 4,)),
            pltpu.SemaphoreType.DMA((levels,)),
            pltpu.SemaphoreType.DMA((slots + 1,)),
        ],
        compiler_params=pltpu.CompilerParams(vmem_limit_bytes=FIRST),
        cost_estimate=pl.CostEstimate(
            flops=4 * width * width * loads, bytes_accessed=2_200_000, transcendentals=0
        ),
    )(targets, rhs_low, inv_low, blocks)


def summed_up(shares, give):
    def body(shares_ref, give_ref, out_ref, same_ref):
        del give_ref, same_ref
        out_ref[...] = jnp.sum(shares_ref[...].astype(F32), axis=0).astype(BF16)

    any_spec, vmem = pl.BlockSpec(memory_space=pl.ANY), pl.BlockSpec(memory_space=pltpu.VMEM)
    return pl.pallas_call(
        body,
        out_shape=(
            jax.ShapeDtypeStruct(shares.shape[1:], BF16),
            jax.ShapeDtypeStruct(give.shape, BF16),
        ),
        in_specs=[vmem, any_spec],
        out_specs=(vmem, any_spec),
        input_output_aliases={1: 1},
        compiler_params=pltpu.CompilerParams(vmem_limit_bytes=SMALL),
        cost_estimate=pl.CostEstimate(flops=200_000, bytes_accessed=450_000, transcendentals=0),
    )(shares, give)


def second_level(part, ready, copies):
    share, width = part.shape

    def body(part_ref, ready_ref, answer_ref, both_ref):
        residual = (ready_ref[:share].astype(F32) - part_ref[...].astype(F32)).astype(BF16)
        answer = dot_nt(residual, ready_ref[2 * share :]).astype(BF16)
        for copy in range(copies):
            answer_ref[copy] = answer
        both_ref[0] = ready_ref[share : 2 * share]
        both_ref[1] = answer

    return pl.pallas_call(
        body,
        out_shape=(
            jax.ShapeDtypeStruct((copies, share, width), BF16),
            jax.ShapeDtypeStruct((2, share, width), BF16),
        ),
        compiler_params=pltpu.CompilerParams(vmem_limit_bytes=SMALL),
        cost_estimate=pl.CostEstimate(
            flops=2 * width * width * share, bytes_accessed=600_000, transcendentals=0
        ),
    )(part, ready)


def ancestor_parts(terms, count, loads, before=None):
    width = terms[0][1].shape[-1]
    arrays = []
    for _, blocks, answer, _ in terms:
        arrays += [array for array in (blocks, answer) if all(array is not held for held in arrays)]
    places = [
        [next(i for i, held in enumerate(arrays) if held is array) for array in term[1:3]]
        for term in terms
    ]

    def body(*refs):
        out_ref = refs[-1]
        for ancestor in range(count):
            columns = slice(ancestor * width, (ancestor + 1) * width)
            total = None
            for (level, _, _, spot), (blocks, answer) in zip(terms, places):
                start = (level * count + ancestor) * width
                product = dot_nt(
                    refs[answer][spot * loads : (spot + 1) * loads],
                    refs[blocks][start : start + width],
                )
                total = product if total is None else total + product
            if before is not None:
                total += refs[len(arrays)][:, columns].astype(F32)
            out_ref[:, columns] = total.astype(BF16)

    operands = arrays if before is None else [*arrays, before]
    vmem = pl.BlockSpec(memory_space=pltpu.VMEM)
    return pl.pallas_call(
        body,
        out_shape=jax.ShapeDtypeStruct((loads, count * width), BF16),
        in_specs=[vmem] * len(operands),
        out_specs=vmem,
        compiler_params=pltpu.CompilerParams(vmem_limit_bytes=LARGE),
        cost_estimate=pl.CostEstimate(
            flops=2 * len(terms) * count * width * width * loads,
            bytes_accessed=5_000_000,
            transcendentals=0,
        ),
    )(*operands)


def ancestor_solve(arrived, rhs_anc, inv_anc):
    sources, loads, _ = arrived.shape
    count, _, width = rhs_anc.shape

    def body(arrived_ref, rhs_ref, inv_ref, out_ref):
        for ancestor in range(count):
            columns = slice(ancestor * width, (ancestor + 1) * width)
            total = jnp.sum(arrived_ref[:, :, columns].astype(F32), axis=0)
            residual = (rhs_ref[ancestor].astype(F32) - total).astype(BF16)
            out_ref[ancestor] = dot_nt(residual, inv_ref[ancestor])

    vmem = pl.BlockSpec(memory_space=pltpu.VMEM)
    return pl.pallas_call(
        body,
        out_shape=jax.ShapeDtypeStruct((count, loads, width), F32),
        in_specs=[vmem] * 3,
        out_specs=vmem,
        compiler_params=pltpu.CompilerParams(vmem_limit_bytes=LARGE),
        cost_estimate=pl.CostEstimate(
            flops=2 * count * width * width * loads, bytes_accessed=3_000_000, transcendentals=0
        ),
    )(arrived, rhs_anc, inv_anc)


def on_device(rhs_low, inv_low, blocks, targets, rhs_anc, inv_anc):
    rows, cols = lax.axis_size("row"), lax.axis_size("col")
    rhs_low, inv_low = rhs_low[0, :, 0], inv_low[0, :, 0]
    blocks, targets = blocks[0, 0, 0], targets[0, 0, 0]
    width, loads = rhs_low.shape[1:]
    layers = lax.axis_size("layer")
    kept = lax.axis_index("layer") & 1

    part, kept0, ready, give = first_level(targets, rhs_low, inv_low, blocks, rows)
    shares = lax.all_to_all(part, "col", 0, 0, tiled=True)

    def neighbour(layer, row):
        ahead = (layer + row) % 2 == 0
        return (layer + (1 if ahead else -1)) % layers

    pairs = [
        (layer * rows + row, neighbour(layer, row) * rows + row)
        for layer in range(layers)
        for row in range(rows)
    ]

    def swap(value):
        return lax.ppermute(value, ("layer", "row"), pairs)

    summed, give = summed_up(shares, give)
    turn = [
        (row * cols + col, col * cols + (row - 1) % rows)
        for row in range(rows)
        for col in range(cols)
    ]
    summed = lax.ppermute(summed, ("row", "col"), turn)
    near = swap(give)
    pieces, both = second_level(summed, ready, rows // 2)
    lines = [list(range(core, rows, 2)) for core in range(2)]
    chips = [[row, row + 1] for row in range(0, rows, 2)]
    pieces = lax.all_to_all(pieces, "row", 0, 0, axis_index_groups=lines, tiled=True)
    answer1 = lax.all_gather(pieces, "row", axis=0, axis_index_groups=chips)

    wanted, count = loads // 2, inv_anc.shape[0]

    def half_of(parity):
        half = lax.dynamic_index_in_dim(answer1, parity, 0, keepdims=False)
        return half.reshape(wanted, width)

    near_answer1 = swap(half_of(1 - kept))
    early = [
        (0, give, kept0, 0),
        (1, give, half_of(kept), 0),
        (0, near, near, near.shape[0] // wanted - 1),
    ]
    parts = ancestor_parts(early, count, wanted)
    parts = ancestor_parts([(1, near, near_answer1, 0)], count, wanted, parts)
    groups = [
        [layer * cols + col for layer in range(parity, layers, 2) for col in range(cols)]
        for parity in range(2)
    ]
    members = len(groups[0])
    arrived = lax.all_to_all(
        parts.reshape(members, parts.shape[0] // members, -1),
        ("layer", "col"),
        0,
        0,
        axis_index_groups=groups,
        tiled=True,
    )
    solved = ancestor_solve(arrived, jnp.swapaxes(rhs_anc, 1, 2), inv_anc)
    return (jnp.swapaxes(both, 1, 2)[None, :, None], jnp.swapaxes(solved, 1, 2))


def solution(mesh):
    in_specs = (
        P("layer", None, "col", None, None),
        P("layer", None, "col", None, None),
        P("layer", "row", "col", None, None, None, None),
        P("layer", "row", "col", None, None),
        P("row", None, ("layer", "col")),
        P("row", None, None),
    )
    out_specs = (P("layer", None, "col", None, "row"), P("row", None, ("layer", "col")))
    return jax.shard_map(
        on_device, mesh=mesh, in_specs=in_specs, out_specs=out_specs, check_vma=False
    )
```

```python
import jax
import jax.numpy as jnp
from jax import lax
from jax.experimental import pallas as pl
from jax.experimental.pallas import tpu as pltpu
from jax.sharding import PartitionSpec as P

F32 = jnp.float32
BF16 = jnp.bfloat16
SMALL = 8 << 20
LARGE = 24 << 20
FIRST = 60 << 20
NT = (((1,), (1,)), ((), ()))


def dot_nt(left, right):
    return lax.dot_general(left, right, NT, preferred_element_type=F32)


def slot_of(targets_ref, level, target, per_row):
    slot, found = jnp.int32(0), jnp.int32(0)
    for member in range(per_row):
        hit = targets_ref[level, member] == target
        slot = jnp.where(hit, jnp.int32(member), slot)
        found = jnp.where(hit, jnp.int32(1), found)
    return slot, found


def first_level(targets, rhs_low, inv_low, blocks, rows):
    levels, width, loads = rhs_low.shape
    per_row = blocks.shape[1]
    share = loads // rows
    steps = 2
    held, half = rows // steps, rows // 2
    slots = levels * per_row
    lanes = max(share, 128)
    per_lanes = lanes // share

    def body(
        lists_ref, rhs_ref, inv_ref, blocks_ref, part_ref, kept_ref, ready_ref, give_ref,
        targets_ref, rhs_in, inv_in, next_in, blocks_in, zeros, half_out, in_sems, blocks_sems, out_sems,
    ):
        kept, row = lax.axis_index("layer") % 2, lax.axis_index("row")
        next_copy = pltpu.make_async_copy(
            rhs_ref.at[1, :, pl.ds(pl.multiple_of(row // per_lanes * lanes, lanes), lanes)],
            next_in,
            in_sems.at[steps + 1],
        )
        next_inverse = pltpu.make_async_copy(
            inv_ref.at[1], ready_ref.at[pl.ds(2 * share, width)], in_sems.at[steps + 2]
        )
        inv_copy = pltpu.make_async_copy(inv_ref.at[0], inv_in, in_sems.at[steps])
        rhs_copies = [
            pltpu.make_async_copy(
                rhs_ref.at[0, :, pl.ds(step * (loads // steps), loads // steps)],
                rhs_in.at[step],
                in_sems.at[step],
            )
            for step in range(steps)
        ]
        blocks_copies = [
            pltpu.make_async_copy(blocks_ref.at[level], blocks_in.at[level], blocks_sems.at[level])
            for level in range(levels)
        ]

        def give(index):
            return give_ref.at[pl.ds(index * width, width)]

        def pass_on(level):
            blocks_copies[level].wait()
            for ancestor in range(per_row):
                index = level * per_row + ancestor
                source, named = slot_of(targets_ref, level, ancestor + 2, per_row)

                @pl.when(named == 1)
                def _(index=index, source=source):
                    pltpu.make_async_copy(
                        blocks_in.at[level, source], give(index), out_sems.at[index]
                    ).start()

                @pl.when(named == 0)
                def _(index=index):
                    pltpu.make_async_copy(zeros, give(index), out_sems.at[index]).start()

        lists_copy = pltpu.make_async_copy(lists_ref, targets_ref, in_sems.at[steps + 3])
        for copy in (inv_copy, *rhs_copies, lists_copy, *blocks_copies, next_copy, next_inverse):
            copy.start()
        zeros[...] = jnp.zeros_like(zeros)
        lists_copy.wait()
        inv_copy.wait()
        answers = []
        for step in range(steps):
            if step > 0:
                pass_on(step - 1)
            rhs_copies[step].wait()
            answer = jnp.dot(inv_in[...], rhs_in[step], preferred_element_type=F32).T.astype(BF16)
            answers.append(answer)
            pieces = [answer[member * share : (member + 1) * share] for member in range(held)]
            for member in range(held):
                start = (step * (held // 2) + member // 2) * share

                @pl.when(kept == member % 2)
                def _(start=start, piece=pieces[member]):
                    kept_ref[start : start + share] = piece

                @pl.when(kept != member % 2)
                def _(start=start, piece=pieces[member]):
                    half_out[start : start + share] = piece

                @pl.when(row == step * held + member)
                def _(piece=pieces[member]):
                    ready_ref[share : 2 * share] = piece

        half_copy = pltpu.make_async_copy(
            half_out, give_ref.at[pl.ds(slots * width, half * share)], out_sems.at[slots]
        )
        half_copy.start()
        for level in range(steps - 1, levels):
            pass_on(level)
        slot, found = slot_of(targets_ref, 0, 1, per_row)

        @pl.when(found == 1)
        def _():
            for step in range(steps):
                part = dot_nt(answers[step], blocks_in[0, slot]).astype(BF16)
                part_ref[step * held : (step + 1) * held] = part.reshape(held, share, width)

        @pl.when(found == 0)
        def _():
            part_ref[...] = jnp.zeros_like(part_ref)

        next_copy.wait()
        turned = next_in[...].astype(F32).T
        picked = turned[:share]
        for other in range(1, per_lanes):
            picked = jnp.where(
                row % per_lanes == other, turned[other * share : (other + 1) * share], picked
            )
        ready_ref[:share] = picked.astype(BF16)
        next_inverse.wait()
        for index in range(slots):
            pltpu.make_async_copy(zeros, give(index), out_sems.at[index]).wait()
        half_copy.wait()

    any_spec, vmem = pl.BlockSpec(memory_space=pl.ANY), pl.BlockSpec(memory_space=pltpu.VMEM)
    return pl.pallas_call(
        body,
        out_shape=(
            jax.ShapeDtypeStruct((rows, share, width), BF16),
            jax.ShapeDtypeStruct((half * share, width), BF16),
            jax.ShapeDtypeStruct((2 * share + width, width), BF16),
            jax.ShapeDtypeStruct((slots * width + half * share, width), BF16),
        ),
        in_specs=[any_spec] * 4,
        out_specs=(vmem, vmem, vmem, any_spec),
        scratch_shapes=[
            pltpu.SMEM(targets.shape, targets.dtype),
            pltpu.VMEM((steps, width, loads // steps), BF16),
            pltpu.VMEM((width, width), BF16),
            pltpu.VMEM((width, lanes), BF16),
            pltpu.VMEM(blocks.shape, BF16),
            pltpu.VMEM((width, width), BF16),
            pltpu.VMEM((half * share, width), BF16),
            pltpu.SemaphoreType.DMA((steps + 4,)),
            pltpu.SemaphoreType.DMA((levels,)),
            pltpu.SemaphoreType.DMA((slots + 1,)),
        ],
        compiler_params=pltpu.CompilerParams(vmem_limit_bytes=FIRST),
        cost_estimate=pl.CostEstimate(
            flops=4 * width * width * loads, bytes_accessed=2_200_000, transcendentals=0
        ),
    )(targets, rhs_low, inv_low, blocks)


def summed_up(shares, give):
    def body(shares_ref, give_ref, out_ref, same_ref):
        del give_ref, same_ref
        out_ref[...] = jnp.sum(shares_ref[...].astype(F32), axis=0).astype(BF16)

    any_spec, vmem = pl.BlockSpec(memory_space=pl.ANY), pl.BlockSpec(memory_space=pltpu.VMEM)
    return pl.pallas_call(
        body,
        out_shape=(
            jax.ShapeDtypeStruct(shares.shape[1:], BF16),
            jax.ShapeDtypeStruct(give.shape, BF16),
        ),
        in_specs=[vmem, any_spec],
        out_specs=(vmem, any_spec),
        input_output_aliases={1: 1},
        compiler_params=pltpu.CompilerParams(vmem_limit_bytes=SMALL),
        cost_estimate=pl.CostEstimate(flops=200_000, bytes_accessed=450_000, transcendentals=0),
    )(shares, give)


def second_level(part, ready, copies):
    share, width = part.shape

    def body(part_ref, ready_ref, answer_ref, both_ref):
        residual = (ready_ref[:share].astype(F32) - part_ref[...].astype(F32)).astype(BF16)
        answer = dot_nt(residual, ready_ref[2 * share :]).astype(BF16)
        for copy in range(copies):
            answer_ref[copy] = answer
        both_ref[0] = ready_ref[share : 2 * share]
        both_ref[1] = answer

    return pl.pallas_call(
        body,
        out_shape=(
            jax.ShapeDtypeStruct((copies, share, width), BF16),
            jax.ShapeDtypeStruct((2, share, width), BF16),
        ),
        compiler_params=pltpu.CompilerParams(vmem_limit_bytes=SMALL),
        cost_estimate=pl.CostEstimate(
            flops=2 * width * width * share, bytes_accessed=600_000, transcendentals=0
        ),
    )(part, ready)


def ancestor_parts(terms, count, loads, before=None):
    width = terms[0][1].shape[-1]
    arrays = []
    for _, blocks, answer, _ in terms:
        arrays += [array for array in (blocks, answer) if all(array is not held for held in arrays)]
    places = [
        [next(i for i, held in enumerate(arrays) if held is array) for array in term[1:3]]
        for term in terms
    ]

    def body(*refs):
        out_ref = refs[-1]
        for ancestor in range(count):
            columns = slice(ancestor * width, (ancestor + 1) * width)
            total = None
            for (level, _, _, spot), (blocks, answer) in zip(terms, places):
                start = (level * count + ancestor) * width
                product = dot_nt(
                    refs[answer][spot * loads : (spot + 1) * loads],
                    refs[blocks][start : start + width],
                )
                total = product if total is None else total + product
            if before is not None:
                total += refs[len(arrays)][:, columns].astype(F32)
            out_ref[:, columns] = total.astype(BF16)

    operands = arrays if before is None else [*arrays, before]
    vmem = pl.BlockSpec(memory_space=pltpu.VMEM)
    return pl.pallas_call(
        body,
        out_shape=jax.ShapeDtypeStruct((loads, count * width), BF16),
        in_specs=[vmem] * len(operands),
        out_specs=vmem,
        compiler_params=pltpu.CompilerParams(vmem_limit_bytes=LARGE),
        cost_estimate=pl.CostEstimate(
            flops=2 * len(terms) * count * width * width * loads,
            bytes_accessed=5_000_000,
            transcendentals=0,
        ),
    )(*operands)


def ancestor_solve(arrived, rhs_anc, inv_anc):
    sources, loads, _ = arrived.shape
    count, _, width = rhs_anc.shape

    def body(arrived_ref, rhs_ref, inv_ref, out_ref):
        for ancestor in range(count):
            columns = slice(ancestor * width, (ancestor + 1) * width)
            total = jnp.sum(arrived_ref[:, :, columns].astype(F32), axis=0)
            residual = (rhs_ref[ancestor].astype(F32) - total).astype(BF16)
            out_ref[ancestor] = dot_nt(residual, inv_ref[ancestor])

    vmem = pl.BlockSpec(memory_space=pltpu.VMEM)
    return pl.pallas_call(
        body,
        out_shape=jax.ShapeDtypeStruct((count, loads, width), F32),
        in_specs=[vmem] * 3,
        out_specs=vmem,
        compiler_params=pltpu.CompilerParams(vmem_limit_bytes=LARGE),
        cost_estimate=pl.CostEstimate(
            flops=2 * count * width * width * loads, bytes_accessed=3_000_000, transcendentals=0
        ),
    )(arrived, rhs_anc, inv_anc)


def on_device(rhs_low, inv_low, blocks, targets, rhs_anc, inv_anc):
    rows, cols = lax.axis_size("row"), lax.axis_size("col")
    rhs_low, inv_low = rhs_low[0, :, 0], inv_low[0, :, 0]
    blocks, targets = blocks[0, 0, 0], targets[0, 0, 0]
    width, loads = rhs_low.shape[1:]
    layers = lax.axis_size("layer")
    kept = lax.axis_index("layer") & 1

    part, kept0, ready, give = first_level(targets, rhs_low, inv_low, blocks, rows)
    shares = lax.all_to_all(part, "col", 0, 0, tiled=True)

    def neighbour(layer, row):
        ahead = (layer + row) % 2 == 0
        return (layer + (1 if ahead else -1)) % layers

    pairs = [
        (layer * rows + row, neighbour(layer, row) * rows + row)
        for layer in range(layers)
        for row in range(rows)
    ]

    def swap(value):
        return lax.ppermute(value, ("layer", "row"), pairs)

    summed, give = summed_up(shares, give)
    turn = [
        (row * cols + col, col * cols + (row - 1) % rows)
        for row in range(rows)
        for col in range(cols)
    ]
    summed = lax.ppermute(summed, ("row", "col"), turn)
    near = swap(give)
    pieces, both = second_level(summed, ready, rows // 2)
    lines = [list(range(core, rows, 2)) for core in range(2)]
    chips = [[row, row + 1] for row in range(0, rows, 2)]
    pieces = lax.all_to_all(pieces, "row", 0, 0, axis_index_groups=lines, tiled=True)
    answer1 = lax.all_gather(pieces, "row", axis=0, axis_index_groups=chips)

    wanted, count = loads // 2, inv_anc.shape[0]

    def half_of(parity):
        half = lax.dynamic_index_in_dim(answer1, parity, 0, keepdims=False)
        return half.reshape(wanted, width)

    near_answer1 = swap(half_of(1 - kept))
    own = [(0, give, kept0, 0), (1, give, half_of(kept), 0)]
    parts = ancestor_parts(own, count, wanted)
    late = [(0, near, near, near.shape[0] // wanted - 1), (1, near, near_answer1, 0)]
    parts = ancestor_parts(late, count, wanted, parts)
    groups = [
        [layer * cols + col for layer in range(parity, layers, 2) for col in range(cols)]
        for parity in range(2)
    ]
    members = len(groups[0])
    arrived = lax.all_to_all(
        parts.reshape(members, parts.shape[0] // members, -1),
        ("layer", "col"),
        0,
        0,
        axis_index_groups=groups,
        tiled=True,
    )
    solved = ancestor_solve(arrived, jnp.swapaxes(rhs_anc, 1, 2), inv_anc)
    return (jnp.swapaxes(both, 1, 2)[None, :, None], jnp.swapaxes(solved, 1, 2))


def solution(mesh):
    in_specs = (
        P("layer", None, "col", None, None),
        P("layer", None, "col", None, None),
        P("layer", "row", "col", None, None, None, None),
        P("layer", "row", "col", None, None),
        P("row", None, ("layer", "col")),
        P("row", None, None),
    )
    out_specs = (P("layer", None, "col", None, "row"), P("row", None, ("layer", "col")))
    return jax.shard_map(
        on_device, mesh=mesh, in_specs=in_specs, out_specs=out_specs, check_vma=False
    )
```
